32 devices in a mesh: slab: 8 (over y, x, core), group: 4 (over z).
Axes of the slice: x: 2, y: 2, z: 4, core: 2. Of those that a mesh axis runs over, the one named last changes fastest.
Arguments:
- grads: bfloat16 [8, 2048, 512], P('group', 'slab'), may hold values from -64 to 64
- grad_slot: int32 [4, 2], P('group'), may hold values from 0 to 1, each once within a row
- momentum: bfloat16 [8, 2048, 512], P('group', 'slab'), may hold values from -6 to 6
Outputs:
- new_momentum: bfloat16 [8, 2048, 512], P('group', 'slab')
- update: bfloat16 [8, 2048, 512], P('group', 'slab')
The draws below stay inside these ranges and needn't reach their ends.
All inputs are finite; a program needn't handle non-finite values.
Results may differ from the reference program's by a relative error of at most 0.0071.
Values may be sent and summed in bfloat16 or wider, within the bound.
No kernel may reach another device: no remote copies, remote signals or barrier semaphores. Data moves between devices by JAX's collectives and lax.ppermute only.
A program may use at most 64 MiB of HBM per device.

```python
import jax
import jax.numpy as jnp
from jax import lax

M = 2048
K = 512
ITERS = 2
E_GRP = 2
EXPERTS = 8
N_GROUP = 4


def draw_grads(key, part):
    key_noise = jax.random.fold_in(key, 0)
    key_rough = jax.random.fold_in(key, 1)
    key_expert = jax.random.fold_in(key, 3)
    key_row = jax.random.fold_in(key, 4)
    expert_pos = jnp.arange(EXPERTS, dtype=jnp.float32) / max(EXPERTS - 1, 1)
    row_pos = jnp.arange(M, dtype=jnp.float32) / (M - 1)
    rough = jnp.exp(jax.random.uniform(key_rough, (EXPERTS, M, 1), minval=-0.5, maxval=0.5))
    expert_blocks = jnp.exp(jax.random.uniform(key_expert, (EXPERTS // E_GRP,), minval=-0.5, maxval=0.5))
    expert_level = jnp.repeat(expert_blocks, E_GRP, total_repeat_length=EXPERTS)
    row_blocks = jnp.exp(jax.random.uniform(key_row, (32,), minval=-0.5, maxval=0.5))
    row_level = jnp.repeat(row_blocks, M // 32, total_repeat_length=M)
    levels = expert_level[:, None, None] * row_level[None, :, None]
    spread = 0.6 * jnp.sqrt((1.0 + 2.0 * expert_pos)[:, None, None] * (1.0 + 2.0 * row_pos)[None, :, None]) * rough * levels
    values = jnp.clip(jax.random.normal(key_noise, (EXPERTS, M, K)), -4.0, 4.0) * spread
    return values.astype(jnp.bfloat16)


def block_levels(rng, shape, cuts, least, largest):
    gain, own = 1.0, jax.random.fold_in(rng, 6)
    for axis_at, blocks in cuts:
        steps = jnp.exp(jax.random.uniform(jax.random.fold_in(own, axis_at), (blocks,), jnp.float32, least / len(cuts), largest / len(cuts)))
        gain = gain * jnp.repeat(steps, shape[axis_at] // blocks).reshape([-1 if axis == axis_at else 1 for axis in range(len(shape))])
    return gain


def gaussian(stream_key, dims, width, bound, cuts=(), held_as=jnp.bfloat16):
    array = jax.random.normal(stream_key, dims, jnp.float32) * width
    if len(cuts) > 0:
        array = block_levels(stream_key, dims, cuts, -0.22, 0.18) * array
    return jnp.clip(array, min=-bound, max=bound).astype(held_as)


def setup_inputs(seed: int = 0) -> dict:
    arg_keys = jax.random.split(jax.random.key(seed), 4)
    grads = draw_grads(jax.random.fold_in(arg_keys[3], 71), 0)
    grad_slot = jax.vmap(lambda own: jax.random.permutation(own, E_GRP))(jax.random.split(arg_keys[1], N_GROUP)).reshape((N_GROUP, E_GRP)).astype(jnp.int32)
    momentum = gaussian(arg_keys[2], (EXPERTS, M, K), 1.0, 6.0, ((0, 4), (1, 8)))
    return dict(grads=grads, grad_slot=grad_slot, momentum=momentum)


COEF_A = 3.4445
COEF_B = -4.775
COEF_C = 2.0315
DECAY_RATE = 0.95

def newton_factor(current):
    identity = jnp.eye(K, dtype=jnp.float32)
    product = current
    for iteration in range(ITERS):
        rounded = current.astype(jnp.bfloat16)
        squared = jnp.dot(rounded, rounded, preferred_element_type=jnp.float32)
        poly = COEF_A * identity + COEF_B * current + COEF_C * squared
        poly_half = poly.astype(jnp.bfloat16)
        if iteration == 0:
            product = poly
        else:
            product = jnp.dot(product.astype(jnp.bfloat16), poly_half, preferred_element_type=jnp.float32)
        if iteration < ITERS - 1:
            halfway = jnp.dot(rounded, poly_half, preferred_element_type=jnp.float32).astype(jnp.bfloat16)
            current = jnp.dot(poly_half, halfway, preferred_element_type=jnp.float32)
    return product

def reference(grads, grad_slot, momentum):
    total_sq = jnp.sum(jnp.square(grads.astype(jnp.float32)))
    root_mean = jnp.sqrt(total_sq / (EXPERTS * M * K) + 1e-06)
    clip_factor = jnp.minimum(1.0, 1.0 / root_mean)
    source_rows = jnp.arange(EXPERTS, dtype=jnp.int32) // E_GRP * E_GRP + grad_slot.reshape(-1).astype(jnp.int32)

    def update_one(pair):
        source, moment = pair
        gradient = lax.dynamic_index_in_dim(grads, source, 0, keepdims=False)
        fresh = (DECAY_RATE * moment.astype(jnp.float32) + clip_factor * gradient.astype(jnp.float32)).astype(jnp.bfloat16)
        gram_matrix = lax.dot_general(fresh, fresh, (((0,), (0,)), ((), ())), preferred_element_type=jnp.float32)
        frobenius = jnp.trace(gram_matrix) + 1e-06
        product = newton_factor(gram_matrix / frobenius)
        scaled_q = (product / jnp.sqrt(frobenius)).astype(jnp.bfloat16)
        result = jnp.sqrt(jnp.float32(M)) * jnp.dot(fresh, scaled_q, preferred_element_type=jnp.float32)
        return (fresh, result.astype(jnp.bfloat16))
    new_momentum, update = lax.map(update_one, (source_rows, momentum))
    return (new_momentum, update)
```

```python
import functools

import jax
import jax.numpy as jnp
from jax import lax
from jax.experimental import pallas as pl
from jax.experimental.pallas import tpu as pltpu
from jax.sharding import PartitionSpec as P

M = 2048
ITERS = 2

COEF_A = 3.4445
COEF_B = -4.775
COEF_C = 2.0315
DECAY_RATE = 0.95

AXES = ("slab", "group")
VMEM_LIMIT = 24 * 1024 * 1024
HALVES = (
    (((1, 0), (2, 0), (2, 1)), (0, 1)),
    (((3, 0), (3, 1), (3, 2)), (2, 3)),
)
BLOCKS = 4
TAIL = 16


def params(semantics=None):
    return pltpu.CompilerParams(vmem_limit_bytes=VMEM_LIMIT, dimension_semantics=semantics)


def cost(flops, bytes_accessed):
    return pl.CostEstimate(flops=flops, bytes_accessed=bytes_accessed, transcendentals=0)


def squares_kernel(grads_ref, out_ref):
    values = grads_ref[...].astype(jnp.float32)
    experts, rows, columns = values.shape
    total = jnp.sum((values * values).reshape(experts * rows, columns), axis=0, keepdims=True)
    lanes = sum(total[:, at : at + 128] for at in range(0, columns, 128))
    out_ref[...] = jnp.broadcast_to(lanes, out_ref.shape)


def sum_squares(grads, copies):
    return pl.pallas_call(
        squares_kernel,
        out_shape=jax.ShapeDtypeStruct((copies, 128), jnp.float32),
        in_specs=[pl.BlockSpec(memory_space=pltpu.VMEM)],
        out_specs=pl.BlockSpec(memory_space=pltpu.VMEM),
        compiler_params=params(),
        cost_estimate=cost(2 * grads.size, 2 * grads.size),
        name="sum_squares",
    )(grads)


def fresh_momentum(momentum, gradient, clip):
    return (
        DECAY_RATE * momentum.astype(jnp.float32) + clip * gradient.astype(jnp.float32)
    ).astype(jnp.bfloat16)


def grid_index(shape):
    return (
        lax.broadcasted_iota(jnp.int32, shape, 0),
        lax.broadcasted_iota(jnp.int32, shape, 1),
    )


def gram_kernel(
    entries, place_ref, squares_ref, m0_ref, g0_ref, m1_ref, g1_ref, pa_ref, pb_ref, clip_ref, rows_ref, gram_ref
):
    total = jnp.sum(squares_ref[...], keepdims=True)
    root_mean = jnp.sqrt(total / entries + 1e-06)
    clip = jnp.minimum(1.0, 1.0 / root_mean)
    clip_ref[...] = jnp.broadcast_to(clip, clip_ref.shape)
    rows = m0_ref.shape[1]
    rows_ref[:rows, :] = fresh_momentum(m0_ref[0], g0_ref[0], clip)
    rows_ref[rows:, :] = fresh_momentum(m1_ref[0], g1_ref[0], clip)
    fresh = rows_ref[...]
    gram_ref[...] = lax.dot_general(
        fresh, fresh, (((0,), (0,)), ((), ())), preferred_element_type=jnp.float32
    )
    size = gram_ref.shape[0] // BLOCKS
    row, column = grid_index((size, size))

    def block(i, j):
        return gram_ref[i * size : (i + 1) * size, j * size : (j + 1) * size]

    for (lower, (first, second)), out_ref in zip(HALVES, (pa_ref, pb_ref)):
        for at, (i, j) in enumerate(lower):
            out_ref[0, at * size : (at + 1) * size, :] = block(i, j).astype(jnp.bfloat16)
        last = block(second, second)
        shared = jnp.where(column <= row, block(first, first), last)
        out_ref[0, 3 * size : 4 * size, :] = shared.astype(jnp.bfloat16)
        diagonal = jnp.sum(jnp.where(column == row, last, 0.0), axis=0, keepdims=True)
        out_ref[0, 4 * size :, :] = jnp.broadcast_to(diagonal, (TAIL, size)).astype(jnp.bfloat16)


def packed_grams(place, squares, momentum, grads, other_momentum, other_grads, entries):
    experts, rows, columns = momentum.shape
    half = experts // 2
    size = columns // BLOCKS
    packed = jax.ShapeDtypeStruct((half, 4 * size + TAIL, size), jnp.bfloat16)
    packed_spec = pl.BlockSpec((1, 4 * size + TAIL, size), lambda i, place: (i, 0, 0))
    by_expert = pl.BlockSpec((1, rows, columns), lambda i, place: (place[0] * half + i, 0, 0))
    by_slot = pl.BlockSpec(
        (1, rows, columns), lambda i, place: (place[1 + place[0] * half + i], 0, 0)
    )
    return pl.pallas_call(
        functools.partial(gram_kernel, entries),
        grid_spec=pltpu.PrefetchScalarGridSpec(
            num_scalar_prefetch=1,
            grid=(half,),
            in_specs=[
                pl.BlockSpec(squares.shape, lambda i, place: (0, 0)),
                by_expert,
                by_slot,
                by_expert,
                by_slot,
            ],
            out_specs=[
                packed_spec,
                packed_spec,
                pl.BlockSpec((8, 128), lambda i, place: (0, 0)),
            ],
            scratch_shapes=[
                pltpu.VMEM((2 * rows, columns), jnp.bfloat16),
                pltpu.VMEM((columns, columns), jnp.float32),
            ],
        ),
        out_shape=[packed, packed, jax.ShapeDtypeStruct((8, 128), jnp.float32)],
        compiler_params=params(("arbitrary",)),
        cost_estimate=cost(
            4 * half * rows * columns * columns, 2 * (4 * half * rows * columns + 2 * packed.size)
        ),
        name="packed_grams",
    )(place, squares, momentum, grads, other_momentum, other_grads)


def momentum_kernel(place_ref, clip_ref, momentum_ref, grads_ref, out_ref):
    out_ref[0] = fresh_momentum(momentum_ref[0], grads_ref[0], clip_ref[:1, :1])


def update_momentum(place, clip, momentum, grads):
    experts, rows, columns = momentum.shape
    by_expert = pl.BlockSpec((1, rows, columns), lambda i, place: (i, 0, 0))
    return pl.pallas_call(
        momentum_kernel,
        grid_spec=pltpu.PrefetchScalarGridSpec(
            num_scalar_prefetch=1,
            grid=(experts,),
            in_specs=[
                pl.BlockSpec(clip.shape, lambda i, place: (0, 0)),
                by_expert,
                pl.BlockSpec((1, rows, columns), lambda i, place: (place[1 + i], 0, 0)),
            ],
            out_specs=by_expert,
        ),
        out_shape=jax.ShapeDtypeStruct(momentum.shape, jnp.bfloat16),
        compiler_params=params(("arbitrary",)),
        cost_estimate=cost(3 * momentum.size, 6 * momentum.size),
        name="update_momentum",
    )(place, clip, momentum, grads)


def bf16_dot(left, right):
    return jnp.dot(left, right, preferred_element_type=jnp.float32)


def newton_kernel(a0_ref, a1_ref, b0_ref, b1_ref, out_ref, frob_ref, gram_ref):
    columns = gram_ref.shape[0]
    size = columns // BLOCKS
    row, column = grid_index((size, size))
    for (lower, (first, second)), (x_ref, y_ref) in zip(
        HALVES, ((a0_ref, a1_ref), (b0_ref, b1_ref))
    ):

        def piece(at, end):
            return x_ref[0, at:end, :].astype(jnp.float32) + y_ref[0, at:end, :].astype(
                jnp.float32
            )

        def put(i, j, value):
            gram_ref[i * size : (i + 1) * size, j * size : (j + 1) * size] = value

        for at, (i, j) in enumerate(lower):
            value = piece(at * size, (at + 1) * size)
            put(i, j, value)
            put(j, i, value.T)
        shared = piece(3 * size, 4 * size)
        flipped = shared.T
        diagonal = piece(4 * size, 4 * size + TAIL)[:1, :]
        put(first, first, jnp.where(column <= row, shared, flipped))
        put(
            second,
            second,
            jnp.where(
                column == row, diagonal, jnp.where(column > row, shared, flipped)
            ),
        )
    row, column = grid_index((columns, columns))
    on_diagonal = row == column
    gram = gram_ref[...]
    frob = jnp.sum(jnp.where(on_diagonal, gram, 0.0), keepdims=True) + 1e-06
    current = gram / frob
    product = None
    for iteration in range(ITERS):
        rounded = current.astype(jnp.bfloat16)
        squared = bf16_dot(rounded, rounded)
        poly = (
            jnp.where(on_diagonal, COEF_A, 0.0) + COEF_B * current + COEF_C * squared
        )
        poly_half = poly.astype(jnp.bfloat16)
        if iteration == 0:
            product = poly
        else:
            product = bf16_dot(product.astype(jnp.bfloat16), poly_half)
        if iteration < ITERS - 1:
            halfway = bf16_dot(rounded, poly_half).astype(jnp.bfloat16)
            current = bf16_dot(poly_half, halfway)
    out_ref[0] = (product / jnp.sqrt(frob)).astype(jnp.bfloat16)


def newton_factors(a0, a1, b0, b1, columns):
    half, depth, size = a0.shape
    packed = pl.BlockSpec((1, depth, size), lambda i: (i, 0, 0))
    return pl.pallas_call(
        newton_kernel,
        grid=(half,),
        in_specs=[packed] * 4,
        out_specs=pl.BlockSpec((1, columns, columns), lambda i: (i, 0, 0)),
        out_shape=jax.ShapeDtypeStruct((half, columns, columns), jnp.bfloat16),
        scratch_shapes=[
            pltpu.VMEM((8, 128), jnp.float32),
            pltpu.VMEM((columns, columns), jnp.float32),
        ],
        compiler_params=params(("arbitrary",)),
        cost_estimate=cost(
            10 * half * columns**3, 2 * (4 * a0.size + half * columns * columns)
        ),
        name="newton_factors",
    )(a0, a1, b0, b1)


def apply_kernel(place_ref, rows_ref, factor_ref, *refs):
    out_ref = refs[-1]
    result = bf16_dot(rows_ref[0], factor_ref[0])
    out_ref[0] = (jnp.sqrt(jnp.float32(M)) * result).astype(jnp.bfloat16)


def apply_factors(place, fresh, factors, update=None):
    experts, rows, columns = fresh.shape
    half = experts // 2
    other = update is not None

    def at_expert(i, place):
        core = 1 - place[0] if other else place[0]
        return (core * half + i, 0, 0)

    return pl.pallas_call(
        apply_kernel,
        grid_spec=pltpu.PrefetchScalarGridSpec(
            num_scalar_prefetch=1,
            grid=(half,),
            in_specs=[
                pl.BlockSpec((1, rows, columns), at_expert),
                pl.BlockSpec((1, columns, columns), lambda i, place: (i, 0, 0)),
            ]
            + ([pl.BlockSpec(memory_space=pl.ANY)] if other else []),
            out_specs=pl.BlockSpec((1, rows, columns), at_expert),
        ),
        out_shape=jax.ShapeDtypeStruct(fresh.shape, jnp.bfloat16),
        input_output_aliases={3: 0} if other else {},
        compiler_params=params(("arbitrary",)),
        cost_estimate=cost(
            2 * half * rows * columns * columns,
            2 * half * (2 * rows * columns + columns * columns),
        ),
        name="apply_other" if other else "apply_own",
    )(*((place, fresh, factors) + ((update,) if other else ())))


def on_device(grads, grad_slot, momentum):
    slab_count = lax.axis_size("slab")
    devices = slab_count * lax.axis_size("group")
    core = lax.axis_index("slab") % 2
    place = jnp.concatenate([core[None].astype(jnp.int32), grad_slot[0].astype(jnp.int32)])

    def swap(value, bit):
        return lax.ppermute(value, "slab", [(i, i ^ bit) for i in range(slab_count)])

    other_grads, other_momentum = swap(grads, 1), swap(momentum, 1)
    squares = lax.all_to_all(sum_squares(grads, devices), AXES, 0, 0, tiled=True)
    a, b, clip = packed_grams(
        place, squares, momentum, grads, other_momentum, other_grads, grads.size * devices
    )
    bits = []
    while 2 << len(bits) < slab_count:
        bits.append(2 << len(bits))
    turned = bits[len(bits) // 2 :] + bits[: len(bits) // 2]
    for step, (bit_a, bit_b) in enumerate(zip(bits, turned)):
        a1, b1 = swap(a, bit_a), swap(b, bit_b)
        if step < len(bits) - 1:
            a = (a.astype(jnp.float32) + a1.astype(jnp.float32)).astype(jnp.bfloat16)
            b = (b.astype(jnp.float32) + b1.astype(jnp.float32)).astype(jnp.bfloat16)
    fresh = update_momentum(place, clip, momentum, grads)
    factors = newton_factors(a, a1, b, b1, grads.shape[2])
    other_factors = swap(factors, 1)
    update = apply_factors(place, fresh, factors)
    update = apply_factors(place, fresh, other_factors, update)
    return (fresh, update)


def solution(mesh):
    in_specs = (P("group", "slab", None), P("group", None), P("group", "slab", None))
    out_specs = (P("group", "slab", None), P("group", "slab", None))
    return jax.shard_map(
        on_device, mesh=mesh, in_specs=in_specs, out_specs=out_specs, check_vma=False
    )
```

```python
import functools

import jax
import jax.numpy as jnp
from jax import lax
from jax.experimental import pallas as pl
from jax.experimental.pallas import tpu as pltpu
from jax.sharding import PartitionSpec as P

M = 2048
ITERS = 2

COEF_A = 3.4445
COEF_B = -4.775
COEF_C = 2.0315
DECAY_RATE = 0.95

AXES = ("slab", "group")
VMEM_LIMIT = 24 * 1024 * 1024
HALVES = (
    (((1, 0), (2, 0), (2, 1)), (0, 1)),
    (((3, 0), (3, 1), (3, 2)), (2, 3)),
)
BLOCKS = 4
TAIL = 16


def params(semantics=None, limit=VMEM_LIMIT):
    return pltpu.CompilerParams(vmem_limit_bytes=limit, dimension_semantics=semantics)


def cost(flops, bytes_accessed):
    return pl.CostEstimate(flops=flops, bytes_accessed=bytes_accessed, transcendentals=0)


def whole(memory_space):
    return pl.BlockSpec(memory_space=memory_space)


def squares_kernel(grads_ref, out_ref, held_ref, arrived):
    chunks = arrived.shape[0]
    depth = held_ref.shape[0] // chunks

    def copy(at):
        rows = pl.ds(at * depth, depth)
        return pltpu.make_async_copy(grads_ref.at[rows], held_ref.at[rows], arrived.at[at])

    for at in range(chunks):
        copy(at).start()
    total = jnp.zeros((8, held_ref.shape[1]), jnp.float32)
    for at in range(chunks):
        copy(at).wait()
        values = held_ref[at * depth : (at + 1) * depth, :].astype(jnp.float32)
        total += jnp.sum((values * values).reshape(depth // 8, 8, -1), axis=0)
    lanes = sum(total[:, at : at + 128] for at in range(0, total.shape[1], 128))
    out_ref[...] = jnp.broadcast_to(jnp.sum(lanes, axis=0, keepdims=True), out_ref.shape)


def sum_squares(grads, copies):
    rows, columns = grads.shape[0] * grads.shape[1], grads.shape[2]
    return pl.pallas_call(
        squares_kernel,
        out_shape=jax.ShapeDtypeStruct((copies, 128), jnp.float32),
        in_specs=[whole(pltpu.HBM)],
        out_specs=whole(pltpu.VMEM),
        scratch_shapes=[
            pltpu.VMEM((rows, columns), grads.dtype),
            pltpu.SemaphoreType.DMA((4,)),
        ],
        compiler_params=params(limit=62 * 1024 * 1024),
        cost_estimate=cost(2 * grads.size, 2 * grads.size),
        name="sum_squares",
    )(grads.reshape(rows, columns))


def select_kernel(slot_ref, order_ref, momentum_ref, grads_ref, mine_ref, theirs_ref, arrived):
    half = mine_ref.shape[0]
    core = lax.axis_index("slab") % 2
    copies = []
    for to, (out_ref, side) in enumerate(((mine_ref, core), (theirs_ref, 1 - core))):
        for i in range(half):
            expert = side * half + i
            for kind, source in enumerate(
                (momentum_ref.at[expert], grads_ref.at[slot_ref[0, expert]])
            ):
                copies.append(
                    pltpu.make_async_copy(
                        source, out_ref.at[i, kind], arrived.at[(to * half + i) * 2 + kind]
                    )
                )
    for copy in copies:
        copy.start()
    for copy in copies:
        copy.wait()


def select_rows(grad_slot, order, momentum, grads):
    experts, rows, columns = momentum.shape
    half = experts // 2
    rows_shape = jax.ShapeDtypeStruct((half, 2, rows, columns), momentum.dtype)
    return pl.pallas_call(
        select_kernel,
        out_shape=[rows_shape, rows_shape],
        in_specs=[
            whole(pltpu.SMEM),
            whole(pltpu.HBM),
            whole(pltpu.HBM),
            whole(pltpu.HBM),
        ],
        out_specs=[whole(pltpu.VMEM)] * 2,
        scratch_shapes=[pltpu.SemaphoreType.DMA((4 * half,))],
        compiler_params=params(),
        cost_estimate=cost(0, 8 * momentum.size),
        name="select_rows",
    )(grad_slot, order, momentum, grads)


def fresh_momentum(momentum, gradient, clip):
    return (
        DECAY_RATE * momentum.astype(jnp.float32) + clip * gradient.astype(jnp.float32)
    ).astype(jnp.bfloat16)


def grid_index(shape):
    return (
        lax.broadcasted_iota(jnp.int32, shape, 0),
        lax.broadcasted_iota(jnp.int32, shape, 1),
    )


def clip_kernel(entries, squares_ref, clip_ref):
    total = jnp.sum(squares_ref[...], keepdims=True)
    root_mean = jnp.sqrt(total / entries + 1e-06)
    clip_ref[...] = jnp.broadcast_to(jnp.minimum(1.0, 1.0 / root_mean), clip_ref.shape)


def clip_factor(squares, entries):
    return pl.pallas_call(
        functools.partial(clip_kernel, entries),
        in_specs=[whole(pltpu.VMEM)],
        out_specs=whole(pltpu.VMEM),
        out_shape=jax.ShapeDtypeStruct((8, 128), jnp.float32),
        compiler_params=params(),
        cost_estimate=cost(2**33, 2**23),
        name="clip_factor",
    )(squares)


def gram_kernel(clip_ref, mine_ref, got_ref, pa_ref, pb_ref, rows_ref, gram_ref):
    clip = clip_ref[:1, :1]
    half, _, rows, columns = mine_ref.shape
    size = columns // BLOCKS
    row, column = grid_index((size, size))

    def block(i, j):
        return gram_ref[i * size : (i + 1) * size, j * size : (j + 1) * size]

    for e in range(half):
        for at, source in enumerate((mine_ref, got_ref)):
            rows_ref[e, at] = fresh_momentum(source[e, 0], source[e, 1], clip)
        fresh = rows_ref[e].reshape(2 * rows, columns)
        gram_ref[...] = lax.dot_general(
            fresh, fresh, (((0,), (0,)), ((), ())), preferred_element_type=jnp.float32
        )
        for (lower, (first, second)), out_ref in zip(HALVES, (pa_ref, pb_ref)):
            for at, (i, j) in enumerate(lower):
                out_ref[e, at * size : (at + 1) * size, :] = block(i, j).astype(jnp.bfloat16)
            last = block(second, second)
            shared = jnp.where(column <= row, block(first, first), last)
            out_ref[e, 3 * size : 4 * size, :] = shared.astype(jnp.bfloat16)
            diagonal = jnp.sum(jnp.where(column == row, last, 0.0), axis=0, keepdims=True)
            out_ref[e, 4 * size :, :] = jnp.broadcast_to(diagonal, (TAIL, size)).astype(
                jnp.bfloat16
            )


def packed_grams(clip, mine, got):
    half, _, rows, columns = mine.shape
    size = columns // BLOCKS
    packed = jax.ShapeDtypeStruct((half, 4 * size + TAIL, size), jnp.bfloat16)
    return pl.pallas_call(
        gram_kernel,
        in_specs=[whole(pltpu.VMEM)] * 3,
        out_specs=[whole(pltpu.VMEM)] * 3,
        out_shape=[
            packed,
            packed,
            jax.ShapeDtypeStruct((half, 2, rows, columns), jnp.bfloat16),
        ],
        scratch_shapes=[pltpu.VMEM((columns, columns), jnp.float32)],
        compiler_params=params(),
        cost_estimate=cost(4 * half * rows * columns * columns, 8 * mine.size),
        name="packed_grams",
    )(clip, mine, got)


def momentum_kernel(clip_ref, rows_ref, theirs_ref, out_ref, made_ref, written):
    half = rows_ref.shape[0]
    core = lax.axis_index("slab") % 2
    copies = [
        pltpu.make_async_copy(rows_ref.at[e, 0], out_ref.at[core * half + e], written.at[0, e])
        for e in range(half)
    ]
    for copy in copies:
        copy.start()
    for e in range(half):
        made_ref[e] = fresh_momentum(theirs_ref[e, 0], theirs_ref[e, 1], clip_ref[:1, :1])
        copy = pltpu.make_async_copy(
            made_ref.at[e], out_ref.at[(1 - core) * half + e], written.at[1, e]
        )
        copy.start()
        copies.append(copy)
    for copy in copies:
        copy.wait()


def update_momentum(clip, rows, theirs):
    half, _, depth, columns = rows.shape
    return pl.pallas_call(
        momentum_kernel,
        in_specs=[whole(pltpu.VMEM)] * 3,
        out_specs=whole(pltpu.HBM),
        out_shape=jax.ShapeDtypeStruct((2 * half, depth, columns), jnp.bfloat16),
        scratch_shapes=[
            pltpu.VMEM((half, depth, columns), jnp.bfloat16),
            pltpu.SemaphoreType.DMA((2, half)),
        ],
        compiler_params=params(),
        cost_estimate=cost(3 * rows.size, 6 * rows.size),
        name="update_momentum",
    )(clip, rows, theirs)


def bf16_dot(left, right):
    return jnp.dot(left, right, preferred_element_type=jnp.float32)


def scaled_rows(rows, factor):
    return (jnp.sqrt(jnp.float32(M)) * bf16_dot(rows, factor)).astype(jnp.bfloat16)


def newton_kernel(a0_ref, a1_ref, b0_ref, b1_ref, rows_ref, factor_ref, send_ref, gram_ref):
    e = pl.program_id(0)
    columns = gram_ref.shape[0]
    size = columns // BLOCKS
    row, column = grid_index((size, size))
    for (lower, (first, second)), (x_ref, y_ref) in zip(
        HALVES, ((a0_ref, a1_ref), (b0_ref, b1_ref))
    ):

        def piece(at, end):
            return x_ref[e, at:end, :].astype(jnp.float32) + y_ref[e, at:end, :].astype(
                jnp.float32
            )

        def put(i, j, value):
            gram_ref[i * size : (i + 1) * size, j * size : (j + 1) * size] = value

        for at, (i, j) in enumerate(lower):
            value = piece(at * size, (at + 1) * size)
            put(i, j, value)
            put(j, i, value.T)
        shared = piece(3 * size, 4 * size)
        flipped = shared.T
        diagonal = piece(4 * size, 4 * size + TAIL)[:1, :]
        put(first, first, jnp.where(column <= row, shared, flipped))
        put(
            second,
            second,
            jnp.where(
                column == row, diagonal, jnp.where(column > row, shared, flipped)
            ),
        )
    row, column = grid_index((columns, columns))
    on_diagonal = row == column
    gram = gram_ref[...]
    frob = jnp.sum(jnp.where(on_diagonal, gram, 0.0), keepdims=True) + 1e-06
    current = gram / frob
    product = None
    for iteration in range(ITERS):
        rounded = current.astype(jnp.bfloat16)
        squared = bf16_dot(rounded, rounded)
        poly = (
            jnp.where(on_diagonal, COEF_A, 0.0) + COEF_B * current + COEF_C * squared
        )
        poly_half = poly.astype(jnp.bfloat16)
        if iteration == 0:
            product = poly
        else:
            product = bf16_dot(product.astype(jnp.bfloat16), poly_half)
        if iteration < ITERS - 1:
            halfway = bf16_dot(rounded, poly_half).astype(jnp.bfloat16)
            current = bf16_dot(poly_half, halfway)
    factor = (product / jnp.sqrt(frob)).astype(jnp.bfloat16)
    factor_ref[e] = factor
    send_ref[e] = scaled_rows(rows_ref[e, 1], factor)


def newton_factors(a0, a1, b0, b1, rows):
    half, _, depth, columns = rows.shape
    return pl.pallas_call(
        newton_kernel,
        grid=(half,),
        in_specs=[whole(pltpu.VMEM)] * 5,
        out_specs=[whole(pltpu.VMEM)] * 2,
        out_shape=[
            jax.ShapeDtypeStruct((half, columns, columns), jnp.bfloat16),
            jax.ShapeDtypeStruct((half, depth, columns), jnp.bfloat16),
        ],
        scratch_shapes=[pltpu.VMEM((columns, columns), jnp.float32)],
        compiler_params=params(("arbitrary",)),
        cost_estimate=cost(
            10 * half * columns**3, 2 * (4 * a0.size + half * columns * columns)
        ),
        name="newton_factors",
    )(a0, a1, b0, b1, rows)


def own_kernel(rows_ref, factor_ref, out_ref, made_ref, written):
    half, depth, _ = made_ref.shape
    pieces = written.shape[1]
    size = depth // pieces
    core = lax.axis_index("slab") % 2
    copies = []
    for e in range(half):
        for piece in range(pieces):
            at = pl.ds(piece * size, size)
            made_ref[e, at] = scaled_rows(rows_ref[e, 0, at], factor_ref[e])
            copies.append(
                pltpu.make_async_copy(
                    made_ref.at[e, at], out_ref.at[core * half + e, at], written.at[e, piece]
                )
            )
            copies[-1].start()
    for copy in copies:
        copy.wait()


def update_own(rows, factors):
    half, _, depth, columns = rows.shape
    return pl.pallas_call(
        own_kernel,
        in_specs=[whole(pltpu.VMEM)] * 2,
        out_specs=whole(pltpu.HBM),
        out_shape=jax.ShapeDtypeStruct((2 * half, depth, columns), jnp.bfloat16),
        scratch_shapes=[
            pltpu.VMEM((half, depth, columns), jnp.bfloat16),
            pltpu.SemaphoreType.DMA((half, 2)),
        ],
        compiler_params=params(),
        cost_estimate=cost(2 * half * depth * columns * columns, 6 * half * depth * columns),
        name="update_own",
    )(rows, factors)


def other_kernel(got_ref, update_ref, out_ref, written):
    half = got_ref.shape[0]
    other = 1 - lax.axis_index("slab") % 2
    copy = pltpu.make_async_copy(got_ref, out_ref.at[pl.ds(other * half, half)], written)
    copy.start()
    copy.wait()


def update_other(got, update):
    return pl.pallas_call(
        other_kernel,
        in_specs=[whole(pltpu.VMEM), whole(pltpu.HBM)],
        out_specs=whole(pltpu.HBM),
        out_shape=jax.ShapeDtypeStruct(update.shape, update.dtype),
        scratch_shapes=[pltpu.SemaphoreType.DMA],
        input_output_aliases={1: 0},
        compiler_params=params(),
        cost_estimate=cost(0, 4 * got.size),
        name="update_other",
    )(got, update)


def add_rounded(left, right):
    return (left.astype(jnp.float32) + right.astype(jnp.float32)).astype(jnp.bfloat16)


def on_device(grads, grad_slot, momentum):
    slab_count = lax.axis_size("slab")
    devices = slab_count * lax.axis_size("group")

    def swap(value, bit):
        return lax.ppermute(value, "slab", [(i, i ^ bit) for i in range(slab_count)])

    partial = sum_squares(grads, devices)
    squares = lax.all_to_all(partial, AXES, 0, 0, tiled=True)
    mine, theirs = select_rows(grad_slot, partial, momentum, grads)
    got = swap(theirs, 1)
    clip = clip_factor(squares, grads.size * devices)
    a, b, rows = packed_grams(clip, mine, got)
    bits = []
    while 2 << len(bits) < slab_count:
        bits.append(2 << len(bits))
    turned = bits[len(bits) // 2 :] + bits[: len(bits) // 2]
    fresh = update_momentum(clip, rows, theirs)
    for step, (bit_a, bit_b) in enumerate(zip(bits, turned)):
        a1, b1 = swap(a, bit_a), swap(b, bit_b)
        if step < len(bits) - 1:
            a, b = add_rounded(a, a1), add_rounded(b, b1)
        if step == 0:
            a, b, fresh = lax.optimization_barrier((a, b, fresh))
    factors, send = newton_factors(a, a1, b, b1, rows)
    update = update_other(swap(send, 1), update_own(rows, factors))
    return (fresh, update)


def solution(mesh):
    in_specs = (P("group", "slab", None), P("group", None), P("group", "slab", None))
    out_specs = (P("group", "slab", None), P("group", "slab", None))
    return jax.shard_map(
        on_device, mesh=mesh, in_specs=in_specs, out_specs=out_specs, check_vma=False
    )
```

```python
import functools

import jax
import jax.numpy as jnp
from jax import lax
from jax.experimental import pallas as pl
from jax.experimental.pallas import tpu as pltpu
from jax.sharding import PartitionSpec as P

M = 2048
ITERS = 2

COEF_A = 3.4445
COEF_B = -4.775
COEF_C = 2.0315
DECAY_RATE = 0.95

AXES = ("slab", "group")
VMEM_LIMIT = 24 * 1024 * 1024
HALVES = (
    (((1, 0), (2, 0), (2, 1)), (0, 1)),
    (((3, 0), (3, 1), (3, 2)), (2, 3)),
)
BLOCKS = 4
TAIL = 16


def params(semantics=None, limit=VMEM_LIMIT):
    return pltpu.CompilerParams(vmem_limit_bytes=limit, dimension_semantics=semantics)


def cost(flops, bytes_accessed):
    return pl.CostEstimate(flops=flops, bytes_accessed=bytes_accessed, transcendentals=0)


def whole(memory_space):
    return pl.BlockSpec(memory_space=memory_space)


def squares_kernel(grads_ref, out_ref):
    values = grads_ref[...].astype(jnp.float32)
    total = jnp.sum((values * values).reshape(values.shape[0] // 8, 8, -1), axis=0)
    lanes = sum(total[:, at : at + 128] for at in range(0, total.shape[1], 128))
    out_ref[...] = jnp.broadcast_to(jnp.sum(lanes, axis=0, keepdims=True), out_ref.shape)


def sum_squares(grads, copies):
    rows, columns = grads.shape[0] * grads.shape[1], grads.shape[2]
    return pl.pallas_call(
        squares_kernel,
        out_shape=jax.ShapeDtypeStruct((copies, 128), jnp.float32),
        in_specs=[whole(pltpu.VMEM)],
        out_specs=whole(pltpu.VMEM),
        compiler_params=params(),
        cost_estimate=cost(2 * grads.size, 2 * grads.size),
        name="sum_squares",
    )(grads.reshape(rows, columns))


def select_kernel(slot_ref, order_ref, momentum_ref, grads_ref, mine_ref, theirs_ref, arrived):
    half = mine_ref.shape[0]
    core = lax.axis_index("slab") % 2
    copies = []
    for to, (out_ref, side) in enumerate(((mine_ref, core), (theirs_ref, 1 - core))):
        for i in range(half):
            expert = side * half + i
            for kind, source in enumerate(
                (momentum_ref.at[expert], grads_ref.at[slot_ref[0, expert]])
            ):
                copies.append(
                    pltpu.make_async_copy(
                        source, out_ref.at[i, kind], arrived.at[(to * half + i) * 2 + kind]
                    )
                )
    for copy in copies:
        copy.start()
    for copy in copies:
        copy.wait()


def select_rows(grad_slot, order, momentum, grads):
    experts, rows, columns = momentum.shape
    half = experts // 2
    rows_shape = jax.ShapeDtypeStruct((half, 2, rows, columns), momentum.dtype)
    return pl.pallas_call(
        select_kernel,
        out_shape=[rows_shape, rows_shape],
        in_specs=[
            whole(pltpu.SMEM),
            whole(pltpu.HBM),
            whole(pltpu.HBM),
            whole(pltpu.HBM),
        ],
        out_specs=[whole(pltpu.VMEM)] * 2,
        scratch_shapes=[pltpu.SemaphoreType.DMA((4 * half,))],
        compiler_params=params(),
        cost_estimate=cost(0, 8 * momentum.size),
        name="select_rows",
    )(grad_slot, order, momentum, grads)


def fresh_momentum(momentum, gradient, clip):
    return (
        DECAY_RATE * momentum.astype(jnp.float32) + clip * gradient.astype(jnp.float32)
    ).astype(jnp.bfloat16)


def grid_index(shape):
    return (
        lax.broadcasted_iota(jnp.int32, shape, 0),
        lax.broadcasted_iota(jnp.int32, shape, 1),
    )


def clip_kernel(entries, squares_ref, clip_ref):
    total = jnp.sum(squares_ref[...], keepdims=True)
    root_mean = jnp.sqrt(total / entries + 1e-06)
    clip_ref[...] = jnp.broadcast_to(jnp.minimum(1.0, 1.0 / root_mean), clip_ref.shape)


def clip_factor(squares, entries):
    return pl.pallas_call(
        functools.partial(clip_kernel, entries),
        in_specs=[whole(pltpu.VMEM)],
        out_specs=whole(pltpu.VMEM),
        out_shape=jax.ShapeDtypeStruct((8, 128), jnp.float32),
        compiler_params=params(),
        cost_estimate=cost(2**33, 2**23),
        name="clip_factor",
    )(squares)


def gram_kernel(clip_ref, mine_ref, got_ref, pa_ref, pb_ref, rows_ref, gram_ref):
    clip = clip_ref[:1, :1]
    half, _, rows, columns = mine_ref.shape
    size = columns // BLOCKS
    row, column = grid_index((size, size))

    def block(i, j):
        return gram_ref[i * size : (i + 1) * size, j * size : (j + 1) * size]

    for e in range(half):
        for at, source in enumerate((mine_ref, got_ref)):
            rows_ref[e, at] = fresh_momentum(source[e, 0], source[e, 1], clip)
        fresh = rows_ref[e].reshape(2 * rows, columns)
        middle = columns // 2
        for rows_at, columns_at in ((0, 0), (middle, 0), (middle, middle)):
            gram_ref[rows_at : rows_at + middle, columns_at : columns_at + middle] = (
                lax.dot_general(
                    fresh[:, rows_at : rows_at + middle],
                    fresh[:, columns_at : columns_at + middle],
                    (((0,), (0,)), ((), ())),
                    preferred_element_type=jnp.float32,
                )
            )
        for (lower, (first, second)), out_ref in zip(HALVES, (pa_ref, pb_ref)):
            for at, (i, j) in enumerate(lower):
                out_ref[e, at * size : (at + 1) * size, :] = block(i, j).astype(jnp.bfloat16)
            last = block(second, second)
            shared = jnp.where(column <= row, block(first, first), last)
            out_ref[e, 3 * size : 4 * size, :] = shared.astype(jnp.bfloat16)
            diagonal = jnp.sum(jnp.where(column == row, last, 0.0), axis=0, keepdims=True)
            out_ref[e, 4 * size :, :] = jnp.broadcast_to(diagonal, (TAIL, size)).astype(
                jnp.bfloat16
            )


def packed_grams(clip, mine, got):
    half, _, rows, columns = mine.shape
    size = columns // BLOCKS
    packed = jax.ShapeDtypeStruct((half, 4 * size + TAIL, size), jnp.bfloat16)
    return pl.pallas_call(
        gram_kernel,
        in_specs=[whole(pltpu.VMEM)] * 3,
        out_specs=[whole(pltpu.VMEM)] * 3,
        out_shape=[
            packed,
            packed,
            jax.ShapeDtypeStruct((half, 2, rows, columns), jnp.bfloat16),
        ],
        scratch_shapes=[pltpu.VMEM((columns, columns), jnp.float32)],
        compiler_params=params(),
        cost_estimate=cost(4 * half * rows * columns * columns, 8 * mine.size),
        name="packed_grams",
    )(clip, mine, got)


def momentum_kernel(clip_ref, rows_ref, theirs_ref, out_ref, made_ref, written):
    half = rows_ref.shape[0]
    core = lax.axis_index("slab") % 2
    copies = [
        pltpu.make_async_copy(rows_ref.at[e, 0], out_ref.at[core * half + e], written.at[0, e])
        for e in range(half)
    ]
    for copy in copies:
        copy.start()
    for e in range(half):
        made_ref[e] = fresh_momentum(theirs_ref[e, 0], theirs_ref[e, 1], clip_ref[:1, :1])
        copy = pltpu.make_async_copy(
            made_ref.at[e], out_ref.at[(1 - core) * half + e], written.at[1, e]
        )
        copy.start()
        copies.append(copy)
    for copy in copies:
        copy.wait()


def update_momentum(clip, rows, theirs):
    half, _, depth, columns = rows.shape
    return pl.pallas_call(
        momentum_kernel,
        in_specs=[whole(pltpu.VMEM)] * 3,
        out_specs=whole(pltpu.HBM),
        out_shape=jax.ShapeDtypeStruct((2 * half, depth, columns), jnp.bfloat16),
        scratch_shapes=[
            pltpu.VMEM((half, depth, columns), jnp.bfloat16),
            pltpu.SemaphoreType.DMA((2, half)),
        ],
        compiler_params=params(),
        cost_estimate=cost(3 * rows.size, 6 * rows.size),
        name="update_momentum",
    )(clip, rows, theirs)


def bf16_dot(left, right):
    return jnp.dot(left, right, preferred_element_type=jnp.float32)


def scaled_rows(rows, factor):
    return (jnp.sqrt(jnp.float32(M)) * bf16_dot(rows, factor)).astype(jnp.bfloat16)


def lower_product(left, right):
    half = left.shape[0] // 2
    return (
        bf16_dot(left[:half], right[:, :half]),
        bf16_dot(left[half:], right[:, :half]),
        bf16_dot(left[half:], right[:, half:]),
    )


def mirrored(parts):
    upper, corner, lower = (part.astype(jnp.bfloat16) for part in parts)
    return jnp.concatenate(
        [
            jnp.concatenate([upper, corner.T], axis=1),
            jnp.concatenate([corner, lower], axis=1),
        ],
        axis=0,
    )


def newton_kernel(a0_ref, a1_ref, b0_ref, b1_ref, rows_ref, factor_ref, send_ref, gram_ref):
    e = pl.program_id(0)
    columns = gram_ref.shape[0]
    size = columns // BLOCKS
    row, column = grid_index((size, size))
    packs = ((a0_ref, a1_ref), (b0_ref, b1_ref))

    def piece(pack, at, end):
        return sum(ref[e, at:end, :].astype(jnp.float32) for ref in pack)

    shared = [piece(pack, 3 * size, 4 * size) for pack in packs]
    diagonal = [piece(pack, 4 * size, 4 * size + TAIL)[:1, :] for pack in packs]
    trace = sum(jnp.sum(jnp.where(column == row, value, 0.0), keepdims=True) for value in shared)
    trace += sum(jnp.sum(value, keepdims=True) for value in diagonal)
    frob = trace + 1e-06
    scale = 1.0 / frob

    def put(i, j, value):
        gram_ref[i * size : (i + 1) * size, j * size : (j + 1) * size] = value

    for at, (lower, (first, second)) in enumerate(HALVES):
        for k, (i, j) in enumerate(lower):
            value = scale * piece(packs[at], k * size, (k + 1) * size)
            put(i, j, value)
            if i // 2 == j // 2:
                put(j, i, value.T)
        value = scale * shared[at]
        flipped = value.T
        put(first, first, jnp.where(column <= row, value, flipped))
        put(
            second,
            second,
            jnp.where(
                column == row,
                scale * diagonal[at],
                jnp.where(column > row, value, flipped),
            ),
        )
    half = columns // 2
    row, column = grid_index((half, half))
    identity = jnp.where(row == column, COEF_A, 0.0)
    current = (gram_ref[:half, :half], gram_ref[half:, :half], gram_ref[half:, half:])
    for iteration in range(ITERS):
        rounded = mirrored(current)
        squared = lower_product(rounded, rounded)
        poly = [COEF_B * x + COEF_C * y for x, y in zip(current, squared)]
        poly_half = mirrored((identity + poly[0], poly[1], identity + poly[2]))
        if iteration == 0:
            product = poly_half
        else:
            product = lower_product(product, poly_half)
            if iteration < ITERS - 1:
                product = mirrored(product)
        if iteration < ITERS - 1:
            halfway = mirrored(lower_product(rounded, poly_half))
            current = lower_product(poly_half, halfway)
    scale = lax.rsqrt(frob)
    factor = mirrored([part * scale for part in product])
    factor_ref[e] = factor
    send_ref[e] = scaled_rows(rows_ref[e, 1], factor)


def newton_factors(a0, a1, b0, b1, rows):
    half, _, depth, columns = rows.shape
    return pl.pallas_call(
        newton_kernel,
        grid=(half,),
        in_specs=[whole(pltpu.VMEM)] * 5,
        out_specs=[whole(pltpu.VMEM)] * 2,
        out_shape=[
            jax.ShapeDtypeStruct((half, columns, columns), jnp.bfloat16),
            jax.ShapeDtypeStruct((half, depth, columns), jnp.bfloat16),
        ],
        scratch_shapes=[pltpu.VMEM((columns, columns), jnp.float32)],
        compiler_params=params(("arbitrary",)),
        cost_estimate=cost(
            10 * half * columns**3, 2 * (4 * a0.size + half * columns * columns)
        ),
        name="newton_factors",
    )(a0, a1, b0, b1, rows)


def own_kernel(rows_ref, factor_ref, out_ref, made_ref, written):
    half, depth, _ = made_ref.shape
    pieces = written.shape[1]
    size = depth // pieces
    core = lax.axis_index("slab") % 2
    copies = []
    for e in range(half):
        for piece in range(pieces):
            at = pl.ds(piece * size, size)
            made_ref[e, at] = scaled_rows(rows_ref[e, 0, at], factor_ref[e])
            copies.append(
                pltpu.make_async_copy(
                    made_ref.at[e, at], out_ref.at[core * half + e, at], written.at[e, piece]
                )
            )
            copies[-1].start()
    for copy in copies:
        copy.wait()


def update_own(rows, factors):
    half, _, depth, columns = rows.shape
    return pl.pallas_call(
        own_kernel,
        in_specs=[whole(pltpu.VMEM)] * 2,
        out_specs=whole(pltpu.HBM),
        out_shape=jax.ShapeDtypeStruct((2 * half, depth, columns), jnp.bfloat16),
        scratch_shapes=[
            pltpu.VMEM((half, depth, columns), jnp.bfloat16),
            pltpu.SemaphoreType.DMA((half, 2)),
        ],
        compiler_params=params(),
        cost_estimate=cost(2 * half * depth * columns * columns, 6 * half * depth * columns),
        name="update_own",
    )(rows, factors)


def other_kernel(got_ref, update_ref, out_ref, written):
    half = got_ref.shape[0]
    other = 1 - lax.axis_index("slab") % 2
    copy = pltpu.make_async_copy(got_ref, out_ref.at[pl.ds(other * half, half)], written)
    copy.start()
    copy.wait()


def update_other(got, update):
    return pl.pallas_call(
        other_kernel,
        in_specs=[whole(pltpu.VMEM), whole(pltpu.HBM)],
        out_specs=whole(pltpu.HBM),
        out_shape=jax.ShapeDtypeStruct(update.shape, update.dtype),
        scratch_shapes=[pltpu.SemaphoreType.DMA],
        input_output_aliases={1: 0},
        compiler_params=params(),
        cost_estimate=cost(0, 4 * got.size),
        name="update_other",
    )(got, update)


def add_rounded(left, right):
    return (left.astype(jnp.float32) + right.astype(jnp.float32)).astype(jnp.bfloat16)


def on_device(grads, grad_slot, momentum):
    slab_count = lax.axis_size("slab")
    devices = slab_count * lax.axis_size("group")

    def swap(value, bit, odd_bit=None):
        odd_bit = odd_bit or bit
        pairs = [(i, i ^ (odd_bit if i % 2 else bit)) for i in range(slab_count)]
        return lax.ppermute(value, "slab", pairs)

    partial = sum_squares(grads, devices)
    squares = lax.all_to_all(partial, AXES, 0, 0, tiled=True)
    mine, theirs = select_rows(grad_slot, partial, momentum, grads)
    got = swap(theirs, 1)
    clip = clip_factor(squares, grads.size * devices)
    a, b, rows = packed_grams(clip, mine, got)
    bits = []
    while 2 << len(bits) < slab_count:
        bits.append(2 << len(bits))
    turned = bits[len(bits) // 2 :] + bits[: len(bits) // 2]
    fresh = update_momentum(clip, rows, theirs)
    for step, (bit_a, bit_b) in enumerate(zip(bits, turned)):
        a1, b1 = swap(a, bit_a), swap(b, bit_b)
        if step < len(bits) - 1:
            a, b = add_rounded(a, a1), add_rounded(b, b1)
        if step == 0:
            a, fresh = lax.optimization_barrier((a, fresh))
    factors, send = newton_factors(a, a1, b, b1, rows)
    update = update_other(swap(send, 1), update_own(rows, factors))
    return (fresh, update)


def solution(mesh):
    in_specs = (P("group", "slab", None), P("group", None), P("group", "slab", None))
    out_specs = (P("group", "slab", None), P("group", "slab", None))
    return jax.shard_map(
        on_device, mesh=mesh, in_specs=in_specs, out_specs=out_specs, check_vma=False
    )
```

```python
import functools

import jax
import jax.numpy as jnp
from jax import lax
from jax.experimental import pallas as pl
from jax.experimental.pallas import tpu as pltpu
from jax.sharding import PartitionSpec as P

M = 2048
ITERS = 2

COEF_A = 3.4445
COEF_B = -4.775
COEF_C = 2.0315
DECAY_RATE = 0.95

AXES = ("slab", "group")
VMEM_LIMIT = 24 * 1024 * 1024
SPREAD = 0.02
HALVES = (
    (((1, 0), (2, 0), (2, 1)), (0, 1)),
    (((3, 0), (3, 1), (3, 2)), (2, 3)),
)
BLOCKS = 4
TAIL = 16


def params(semantics=None, limit=VMEM_LIMIT):
    return pltpu.CompilerParams(vmem_limit_bytes=limit, dimension_semantics=semantics)


def cost(flops, bytes_accessed):
    return pl.CostEstimate(flops=flops, bytes_accessed=bytes_accessed, transcendentals=0)


def whole(memory_space):
    return pl.BlockSpec(memory_space=memory_space)


def squares_kernel(grads_ref, slot_ref, out_ref, slots_ref):
    slots_ref[...] = slot_ref[...]
    values = grads_ref[...].astype(jnp.float32)
    total = jnp.sum((values * values).reshape(values.shape[0] // 8, 8, -1), axis=0)
    lanes = sum(total[:, at : at + 128] for at in range(0, total.shape[1], 128))
    out_ref[...] = jnp.broadcast_to(jnp.sum(lanes, axis=0, keepdims=True), out_ref.shape)


def sum_squares(grads, grad_slot, copies):
    rows, columns = grads.shape[0] * grads.shape[1], grads.shape[2]
    return pl.pallas_call(
        squares_kernel,
        out_shape=[
            jax.ShapeDtypeStruct((copies, 128), jnp.float32),
            jax.ShapeDtypeStruct(grad_slot.shape, jnp.int32),
        ],
        in_specs=[whole(pltpu.VMEM)] * 2,
        out_specs=[whole(pltpu.VMEM)] * 2,
        compiler_params=params(),
        cost_estimate=cost(2 * grads.size, 2 * grads.size),
        name="sum_squares",
    )(grads.reshape(rows, columns), grad_slot)


def slot_gradient(slots, expert, grads_ref):
    lane = lax.broadcasted_iota(jnp.int32, slots.shape, 1)
    slot = jnp.sum(jnp.where(lane == expert, slots, 0), axis=1, keepdims=True)
    gradient = grads_ref[0]
    for at in range(1, grads_ref.shape[0]):
        gradient = jnp.where(slot == at, grads_ref[at], gradient)
    return gradient


def fresh_momentum(momentum, gradient, clip):
    return (
        DECAY_RATE * momentum.astype(jnp.float32) + clip * gradient.astype(jnp.float32)
    ).astype(jnp.bfloat16)


def grid_index(shape):
    return (
        lax.broadcasted_iota(jnp.int32, shape, 0),
        lax.broadcasted_iota(jnp.int32, shape, 1),
    )


def pack_gram(e, rows_ref, pa_ref, pb_ref, gram_ref):
    _, _, rows, columns = rows_ref.shape
    size = columns // BLOCKS
    row, column = grid_index((size, size))
    fresh = rows_ref[e].reshape(2 * rows, columns)
    middle = columns // 2
    for rows_at, columns_at in ((0, 0), (middle, 0), (middle, middle)):
        gram_ref[rows_at : rows_at + middle, columns_at : columns_at + middle] = lax.dot_general(
            fresh[:, rows_at : rows_at + middle],
            fresh[:, columns_at : columns_at + middle],
            (((0,), (0,)), ((), ())),
            preferred_element_type=jnp.float32,
        )

    def block(i, j):
        return gram_ref[i * size : (i + 1) * size, j * size : (j + 1) * size]

    for (lower, (first, second)), out_ref in zip(HALVES, (pa_ref, pb_ref)):
        for at, (i, j) in enumerate(lower):
            out_ref[e, at * size : (at + 1) * size, :] = block(i, j).astype(out_ref.dtype)
        last = block(second, second)
        shared = jnp.where(column <= row, block(first, first), last)
        out_ref[e, 3 * size : 4 * size, :] = shared.astype(out_ref.dtype)
        diagonal = jnp.sum(jnp.where(column == row, last, 0.0), axis=0, keepdims=True)
        out_ref[e, 4 * size :, :] = jnp.broadcast_to(diagonal, (TAIL, size)).astype(
            out_ref.dtype
        )


def exact_grams_kernel(rows_ref, pa_ref, pb_ref, gram_ref):
    pack_gram(pl.program_id(0), rows_ref, pa_ref, pb_ref, gram_ref)


def exact_grams(rows):
    half, _, depth, columns = rows.shape
    size = columns // BLOCKS
    packed = jax.ShapeDtypeStruct((half, 4 * size + TAIL, size), jnp.float32)
    return pl.pallas_call(
        exact_grams_kernel,
        grid=(half,),
        in_specs=[whole(pltpu.VMEM)],
        out_specs=[whole(pltpu.VMEM)] * 2,
        out_shape=[packed, packed],
        scratch_shapes=[pltpu.VMEM((columns, columns), jnp.float32)],
        compiler_params=params(("arbitrary",)),
        cost_estimate=cost(4 * half * depth * columns * columns, 4 * rows.size),
        name="exact_grams",
    )(rows)


def gram_kernel(
    entries, squares_ref, slot_ref, m_ref, g_ref, om_ref, og_ref,
    pa_ref, pb_ref, rows_ref, clip_ref, gram_ref,
):
    total = jnp.sum(squares_ref[...], keepdims=True)
    root_mean = jnp.sqrt(total / entries + 1e-06)
    clip = jnp.minimum(1.0, 1.0 / root_mean)
    clip_ref[...] = jnp.broadcast_to(clip, clip_ref.shape)
    half = m_ref.shape[0] // 2
    core = lax.axis_index("slab") % 2
    for e in range(half):
        expert = core * half + e
        for at, (momentum_ref, grads_ref) in enumerate(((m_ref, g_ref), (om_ref, og_ref))):
            rows_ref[e, at] = fresh_momentum(
                momentum_ref[expert], slot_gradient(slot_ref[...], expert, grads_ref), clip
            )
        pack_gram(e, rows_ref, pa_ref, pb_ref, gram_ref)


def packed_grams(squares, grad_slot, momentum, grads, other_momentum, other_grads, entries):
    experts, rows, columns = momentum.shape
    half = experts // 2
    size = columns // BLOCKS
    packed = jax.ShapeDtypeStruct((half, 4 * size + TAIL, size), jnp.bfloat16)
    return pl.pallas_call(
        functools.partial(gram_kernel, entries),
        in_specs=[whole(pltpu.VMEM)] * 6,
        out_specs=[whole(pltpu.VMEM)] * 4,
        out_shape=[
            packed,
            packed,
            jax.ShapeDtypeStruct((half, 2, rows, columns), jnp.bfloat16),
            jax.ShapeDtypeStruct((8, 128), jnp.float32),
        ],
        scratch_shapes=[pltpu.VMEM((columns, columns), jnp.float32)],
        compiler_params=params(),
        cost_estimate=cost(4 * half * rows * columns * columns, 8 * momentum.size),
        name="packed_grams",
    )(squares, grad_slot, momentum, grads, other_momentum, other_grads)


def momentum_kernel(slot_ref, clip_ref, rows_ref, m_ref, g_ref, out_ref, made_ref, written):
    half = rows_ref.shape[0]
    core = lax.axis_index("slab") % 2
    copies = [
        pltpu.make_async_copy(rows_ref.at[e, 0], out_ref.at[core * half + e], written.at[0, e])
        for e in range(half)
    ]
    for copy in copies:
        copy.start()
    for e in range(half):
        expert = (1 - core) * half + e
        made_ref[e] = fresh_momentum(
            m_ref[expert], slot_gradient(slot_ref[...], expert, g_ref), clip_ref[:1, :1]
        )
        copy = pltpu.make_async_copy(made_ref.at[e], out_ref.at[expert], written.at[1, e])
        copy.start()
        copies.append(copy)
    for copy in copies:
        copy.wait()


def update_momentum(grad_slot, clip, rows, momentum, grads):
    half, _, depth, columns = rows.shape
    return pl.pallas_call(
        momentum_kernel,
        in_specs=[whole(pltpu.VMEM)] * 5,
        out_specs=whole(pltpu.HBM),
        out_shape=jax.ShapeDtypeStruct((2 * half, depth, columns), jnp.bfloat16),
        scratch_shapes=[
            pltpu.VMEM((half, depth, columns), jnp.bfloat16),
            pltpu.SemaphoreType.DMA((2, half)),
        ],
        compiler_params=params(),
        cost_estimate=cost(3 * rows.size, 6 * rows.size),
        name="update_momentum",
    )(grad_slot, clip, rows, momentum, grads)


def bf16_dot(left, right):
    return jnp.dot(left, right, preferred_element_type=jnp.float32)


def scaled_rows(rows, factor):
    return (jnp.sqrt(jnp.float32(M)) * bf16_dot(rows, factor)).astype(jnp.bfloat16)


def lower_product(left, right):
    half = left.shape[0] // 2
    return (
        bf16_dot(left[:half], right[:, :half]),
        bf16_dot(left[half:], right[:, :half]),
        bf16_dot(left[half:], right[:, half:]),
    )


def mirrored(parts):
    upper, corner, lower = (part.astype(jnp.bfloat16) for part in parts)
    return jnp.concatenate(
        [
            jnp.concatenate([upper, corner.T], axis=1),
            jnp.concatenate([corner, lower], axis=1),
        ],
        axis=0,
    )


def unpack_scaled(e, packs, gram_ref, whole_matrix):
    columns = gram_ref.shape[0]
    size = columns // BLOCKS
    row, column = grid_index((size, size))

    def piece(pack, at, end):
        return sum(ref[e, at:end, :].astype(jnp.float32) for ref in pack)

    shared = [piece(pack, 3 * size, 4 * size) for pack in packs]
    diagonal = [piece(pack, 4 * size, 4 * size + TAIL)[:1, :] for pack in packs]
    trace = sum(jnp.sum(jnp.where(column == row, value, 0.0), keepdims=True) for value in shared)
    trace += sum(jnp.sum(value, keepdims=True) for value in diagonal)
    frob = trace + 1e-06
    scale = 1.0 / frob

    def put(i, j, value):
        gram_ref[i * size : (i + 1) * size, j * size : (j + 1) * size] = value

    for at, (lower, (first, second)) in enumerate(HALVES):
        for k, (i, j) in enumerate(lower):
            value = scale * piece(packs[at], k * size, (k + 1) * size)
            put(i, j, value)
            if whole_matrix or i // 2 == j // 2:
                put(j, i, value.T)
        value = scale * shared[at]
        flipped = value.T
        put(first, first, jnp.where(column <= row, value, flipped))
        put(
            second,
            second,
            jnp.where(
                column == row,
                scale * diagonal[at],
                jnp.where(column > row, value, flipped),
            ),
        )
    return frob


def newton_kernel(
    a0_ref, a1_ref, b0_ref, b1_ref, rows_ref, factor_ref, send_ref, narrow_ref, gram_ref
):
    e = pl.program_id(0)
    columns = gram_ref.shape[0]
    frob = unpack_scaled(e, ((a0_ref, a1_ref), (b0_ref, b1_ref)), gram_ref, False)
    half = columns // 2
    row, column = grid_index((half, half))
    identity = jnp.where(row == column, COEF_A, 0.0)
    current = (gram_ref[:half, :half], gram_ref[half:, :half], gram_ref[half:, half:])
    for iteration in range(ITERS):
        rounded = mirrored(current)
        squared = lower_product(rounded, rounded)
        if iteration == 0:
            spread = jnp.sum(jnp.where(row == column, squared[0] + squared[2], 0.0), keepdims=True)
            narrow = jnp.where(spread > SPREAD, 1.0, 0.0)
            narrow_ref[e] = jnp.broadcast_to(narrow, narrow_ref.shape[1:])
        poly = [COEF_B * x + COEF_C * y for x, y in zip(current, squared)]
        poly_half = mirrored((identity + poly[0], poly[1], identity + poly[2]))
        if iteration == 0:
            product = poly_half
        else:
            product = lower_product(product, poly_half)
            if iteration < ITERS - 1:
                product = mirrored(product)
        if iteration < ITERS - 1:
            halfway = mirrored(lower_product(rounded, poly_half))
            current = lower_product(poly_half, halfway)
    scale = lax.rsqrt(frob)
    factor = mirrored([part * scale for part in product])
    factor_ref[e] = factor
    depth = rows_ref.shape[2]
    send_ref[e, :depth] = scaled_rows(rows_ref[e, 1], factor)
    send_ref[e, depth:] = jnp.broadcast_to(narrow, (TAIL, columns)).astype(jnp.bfloat16)


def exact_newton_kernel(
    a0_ref, a1_ref, b0_ref, b1_ref, rows_ref, factor_ref, send_ref, gram_ref
):
    e = pl.program_id(0)
    frob = unpack_scaled(e, ((a0_ref, a1_ref), (b0_ref, b1_ref)), gram_ref, True)
    row, column = grid_index(gram_ref.shape)
    identity = jnp.where(row == column, COEF_A, 0.0)
    current = gram_ref[...]
    for iteration in range(ITERS):
        rounded = current.astype(jnp.bfloat16)
        poly = identity + COEF_B * current + COEF_C * bf16_dot(rounded, rounded)
        poly_half = poly.astype(jnp.bfloat16)
        if iteration == 0:
            product = poly
        else:
            product = bf16_dot(product.astype(jnp.bfloat16), poly_half)
        if iteration < ITERS - 1:
            halfway = bf16_dot(rounded, poly_half).astype(jnp.bfloat16)
            current = bf16_dot(poly_half, halfway)
    factor = (product / jnp.sqrt(frob)).astype(jnp.bfloat16)
    factor_ref[e] = factor
    send_ref[e] = scaled_rows(rows_ref[e, 1], factor)


def newton_factors(a0, a1, b0, b1, rows, exact):
    half, _, depth, columns = rows.shape
    narrow = [] if exact else [jax.ShapeDtypeStruct((half, 8, 128), jnp.float32)]
    return pl.pallas_call(
        exact_newton_kernel if exact else newton_kernel,
        grid=(half,),
        in_specs=[whole(pltpu.VMEM)] * 5,
        out_specs=[whole(pltpu.VMEM)] * (2 + len(narrow)),
        out_shape=[
            jax.ShapeDtypeStruct((half, columns, columns), jnp.bfloat16),
            jax.ShapeDtypeStruct((half, depth + (0 if exact else TAIL), columns), jnp.bfloat16),
        ]
        + narrow,
        scratch_shapes=[pltpu.VMEM((columns, columns), jnp.float32)],
        compiler_params=params(("arbitrary",)),
        cost_estimate=cost(
            10 * half * columns**3, 2 * (4 * a0.size + half * columns * columns)
        ),
        name="exact_newton" if exact else "newton_factors",
    )(a0, a1, b0, b1, rows)


def own_kernel(rows_ref, factor_ref, *refs):
    out_ref, made_ref, written = refs[-3:]
    half, depth, _ = made_ref.shape
    pieces = written.shape[1]
    size = depth // pieces
    core = lax.axis_index("slab") % 2
    copies = []
    for e in range(half):
        for piece in range(pieces):
            at = pl.ds(piece * size, size)
            made_ref[e, at] = scaled_rows(rows_ref[e, 0, at], factor_ref[e])
            copies.append(
                pltpu.make_async_copy(
                    made_ref.at[e, at], out_ref.at[core * half + e, at], written.at[e, piece]
                )
            )
            copies[-1].start()
    for copy in copies:
        copy.wait()


def update_own(rows, factors, update=None):
    into = () if update is None else (update,)
    half, _, depth, columns = rows.shape
    return pl.pallas_call(
        own_kernel,
        in_specs=[whole(pltpu.VMEM)] * 2 + [whole(pltpu.HBM)] * len(into),
        out_specs=whole(pltpu.HBM),
        out_shape=pltpu.HBM((2 * half, depth, columns), jnp.bfloat16),
        scratch_shapes=[
            pltpu.VMEM((half, depth, columns), jnp.bfloat16),
            pltpu.SemaphoreType.DMA((half, 2)),
        ],
        input_output_aliases={2: 0} if into else {},
        compiler_params=params(),
        cost_estimate=cost(2 * half * depth * columns * columns, 6 * half * depth * columns),
        name="update_own",
    )(rows, factors, *into)


def other_kernel(got_ref, update_ref, out_ref, written):
    half, depth = got_ref.shape[0], out_ref.shape[1]
    other = 1 - lax.axis_index("slab") % 2
    copy = pltpu.make_async_copy(
        got_ref.at[:, pl.ds(0, depth)], out_ref.at[pl.ds(other * half, half)], written
    )
    copy.start()
    return copy


def plain_other_kernel(got_ref, update_ref, out_ref, written):
    other_kernel(got_ref, update_ref, out_ref, written).wait()


def flag_other_kernel(got_ref, update_ref, narrow_ref, out_ref, flag_ref, written):
    copy = other_kernel(got_ref, update_ref, out_ref, written)
    own = jnp.max(jnp.max(narrow_ref[...], axis=0), keepdims=True)
    tails = got_ref[:, got_ref.shape[1] - TAIL :, :128].astype(jnp.float32)
    flag_ref[0, 0] = jnp.max(jnp.maximum(own, jnp.max(jnp.max(tails, axis=0), keepdims=True)))
    copy.wait()


def update_other(got, update, narrow=None):
    written = pltpu.HBM(update.shape, update.dtype)
    common = dict(
        scratch_shapes=[pltpu.SemaphoreType.DMA],
        input_output_aliases={1: 0},
        compiler_params=params(),
        cost_estimate=cost(0, 4 * got.size),
    )
    if narrow is None:
        return pl.pallas_call(
            plain_other_kernel,
            in_specs=[whole(pltpu.VMEM), whole(pltpu.HBM)],
            out_specs=whole(pltpu.HBM),
            out_shape=written,
            name="update_other",
            **common,
        )(got, update)
    return pl.pallas_call(
        flag_other_kernel,
        in_specs=[whole(pltpu.VMEM), whole(pltpu.HBM), whole(pltpu.VMEM)],
        out_specs=[whole(pltpu.HBM), whole(pltpu.SMEM)],
        out_shape=[written, pltpu.SMEM((1, 1), jnp.float32)],
        name="update_other_flag",
        **common,
    )(got, update, narrow)


def add_rounded(left, right):
    return (left.astype(jnp.float32) + right.astype(jnp.float32)).astype(left.dtype)


def on_device(grads, grad_slot, momentum):
    slab_count = lax.axis_size("slab")
    devices = slab_count * lax.axis_size("group")

    def swap(value, bit, odd_bit=None):
        odd_bit = odd_bit or bit
        pairs = [(i, i ^ (odd_bit if i % 2 else bit)) for i in range(slab_count)]
        return lax.ppermute(value, "slab", pairs)

    partial, grad_slot = sum_squares(grads, grad_slot, devices)
    other_momentum, other_grads = swap(momentum, 1), swap(grads, 1)
    squares = lax.all_to_all(partial, AXES, 0, 0, tiled=True)
    a, b, rows, clip = packed_grams(
        squares, grad_slot, momentum, grads, other_momentum, other_grads, grads.size * devices
    )
    bits = []
    while 2 << len(bits) < slab_count:
        bits.append(2 << len(bits))
    turned = bits[len(bits) // 2 :] + bits[: len(bits) // 2]

    def added_up(a, b, beside=None):
        for step, (bit_a, bit_b) in enumerate(zip(bits, turned)):
            a1, b1 = swap(a, bit_a), swap(b, bit_b)
            if step < len(bits) - 1:
                a, b = add_rounded(a, a1), add_rounded(b, b1)
            if step == 0 and beside is not None:
                a, beside = lax.optimization_barrier((a, beside))
        return (a, a1, b, b1), beside

    fresh = update_momentum(grad_slot, clip, rows, momentum, grads)
    terms, fresh = added_up(a, b, fresh)
    factors, send, narrow = newton_factors(*terms, rows, exact=False)
    got = swap(send, 1)
    update, flag = update_other(got, update_own(rows, factors), narrow)

    def narrow_update(rows, update):
        terms, _ = added_up(*exact_grams(rows))
        factors, send = newton_factors(*terms, rows, exact=True)
        return update_other(swap(send, 1), update_own(rows, factors, update))

    def spread_update(rows, update):
        return update

    update = lax.cond(flag[0, 0] > 0.0, narrow_update, spread_update, rows, update)
    return (fresh, update)


def solution(mesh):
    in_specs = (P("group", "slab", None), P("group", None), P("group", "slab", None))
    out_specs = (P("group", "slab", None), P("group", "slab", None))
    return jax.shard_map(
        on_device, mesh=mesh, in_specs=in_specs, out_specs=out_specs, check_vma=False
    )
```

```python
import functools

import jax
import jax.numpy as jnp
from jax import lax
from jax.experimental import pallas as pl
from jax.experimental.pallas import tpu as pltpu
from jax.sharding import PartitionSpec as P

M = 2048
ITERS = 2

COEF_A = 3.4445
COEF_B = -4.775
COEF_C = 2.0315
DECAY_RATE = 0.95

AXES = ("slab", "group")
VMEM_LIMIT = 24 * 1024 * 1024
SPREAD = 0.02
HALVES = (
    (((1, 0), (2, 0), (2, 1)), (0, 1)),
    (((3, 0), (3, 1), (3, 2)), (2, 3)),
)
BLOCKS = 4
TAIL = 16


def params(semantics=None, limit=VMEM_LIMIT):
    return pltpu.CompilerParams(vmem_limit_bytes=limit, dimension_semantics=semantics)


def cost(flops, bytes_accessed):
    return pl.CostEstimate(flops=flops, bytes_accessed=bytes_accessed, transcendentals=0)


def whole(memory_space):
    return pl.BlockSpec(memory_space=memory_space)


def squares_kernel(grads_ref, slot_ref, out_ref, slots_ref):
    slots_ref[...] = slot_ref[...]
    values = grads_ref[...].astype(jnp.float32)
    total = jnp.sum((values * values).reshape(values.shape[0] // 8, 8, -1), axis=0)
    lanes = sum(total[:, at : at + 128] for at in range(0, total.shape[1], 128))
    out_ref[...] = jnp.broadcast_to(jnp.sum(lanes, axis=0, keepdims=True), out_ref.shape)


def sum_squares(grads, grad_slot, copies):
    rows, columns = grads.shape[0] * grads.shape[1], grads.shape[2]
    return pl.pallas_call(
        squares_kernel,
        out_shape=[
            jax.ShapeDtypeStruct((copies, 128), jnp.float32),
            jax.ShapeDtypeStruct(grad_slot.shape, jnp.int32),
        ],
        in_specs=[whole(pltpu.VMEM)] * 2,
        out_specs=[whole(pltpu.VMEM)] * 2,
        compiler_params=params(),
        cost_estimate=cost(2 * grads.size, 2 * grads.size),
        name="sum_squares",
    )(grads.reshape(rows, columns), grad_slot)


def slot_gradient(slots, expert, grads_ref):
    lane = lax.broadcasted_iota(jnp.int32, slots.shape, 1)
    slot = jnp.sum(jnp.where(lane == expert, slots, 0), axis=1, keepdims=True)
    gradient = grads_ref[0]
    for at in range(1, grads_ref.shape[0]):
        gradient = jnp.where(slot == at, grads_ref[at], gradient)
    return gradient


def fresh_momentum(momentum, gradient, clip):
    return (
        DECAY_RATE * momentum.astype(jnp.float32) + clip * gradient.astype(jnp.float32)
    ).astype(jnp.bfloat16)


def grid_index(shape):
    return (
        lax.broadcasted_iota(jnp.int32, shape, 0),
        lax.broadcasted_iota(jnp.int32, shape, 1),
    )


def pack_gram(e, rows_ref, pa_ref, pb_ref, gram_ref):
    _, _, rows, columns = rows_ref.shape
    size = columns // BLOCKS
    row, column = grid_index((size, size))
    fresh = rows_ref[e].reshape(2 * rows, columns)
    middle = columns // 2
    for rows_at, columns_at in ((0, 0), (middle, 0), (middle, middle)):
        gram_ref[rows_at : rows_at + middle, columns_at : columns_at + middle] = lax.dot_general(
            fresh[:, rows_at : rows_at + middle],
            fresh[:, columns_at : columns_at + middle],
            (((0,), (0,)), ((), ())),
            preferred_element_type=jnp.float32,
        )

    def block(i, j):
        return gram_ref[i * size : (i + 1) * size, j * size : (j + 1) * size]

    for (lower, (first, second)), out_ref in zip(HALVES, (pa_ref, pb_ref)):
        for at, (i, j) in enumerate(lower):
            out_ref[e, at * size : (at + 1) * size, :] = block(i, j).astype(out_ref.dtype)
        last = block(second, second)
        shared = jnp.where(column <= row, block(first, first), last)
        out_ref[e, 3 * size : 4 * size, :] = shared.astype(out_ref.dtype)
        diagonal = jnp.sum(jnp.where(column == row, last, 0.0), axis=0, keepdims=True)
        out_ref[e, 4 * size :, :] = jnp.broadcast_to(diagonal, (TAIL, size)).astype(
            out_ref.dtype
        )


def exact_grams_kernel(rows_ref, pa_ref, pb_ref, gram_ref):
    pack_gram(pl.program_id(0), rows_ref, pa_ref, pb_ref, gram_ref)


def exact_grams(rows):
    half, _, depth, columns = rows.shape
    size = columns // BLOCKS
    packed = jax.ShapeDtypeStruct((half, 4 * size + TAIL, size), jnp.float32)
    return pl.pallas_call(
        exact_grams_kernel,
        grid=(half,),
        in_specs=[whole(pltpu.VMEM)],
        out_specs=[whole(pltpu.VMEM)] * 2,
        out_shape=[packed, packed],
        scratch_shapes=[pltpu.VMEM((columns, columns), jnp.float32)],
        compiler_params=params(("arbitrary",)),
        cost_estimate=cost(4 * half * depth * columns * columns, 4 * rows.size),
        name="exact_grams",
    )(rows)


def gram_kernel(
    entries, squares_ref, slot_ref, m_ref, g_ref, om_ref, og_ref,
    pa_ref, pb_ref, rows_ref, clip_ref, gram_ref,
):
    total = jnp.sum(squares_ref[...], keepdims=True)
    root_mean = jnp.sqrt(total / entries + 1e-06)
    clip = jnp.minimum(1.0, 1.0 / root_mean)
    clip_ref[...] = jnp.broadcast_to(clip, clip_ref.shape)
    half = m_ref.shape[0] // 2
    core = lax.axis_index("slab") % 2
    for e in range(half):
        expert = core * half + e
        for at, (momentum_ref, grads_ref) in enumerate(((m_ref, g_ref), (om_ref, og_ref))):
            rows_ref[e, at] = fresh_momentum(
                momentum_ref[expert], slot_gradient(slot_ref[...], expert, grads_ref), clip
            )
        pack_gram(e, rows_ref, pa_ref, pb_ref, gram_ref)


def packed_grams(squares, grad_slot, momentum, grads, other_momentum, other_grads, entries):
    experts, rows, columns = momentum.shape
    half = experts // 2
    size = columns // BLOCKS
    packed = jax.ShapeDtypeStruct((half, 4 * size + TAIL, size), jnp.bfloat16)
    return pl.pallas_call(
        functools.partial(gram_kernel, entries),
        in_specs=[whole(pltpu.VMEM)] * 6,
        out_specs=[whole(pltpu.VMEM)] * 4,
        out_shape=[
            packed,
            packed,
            jax.ShapeDtypeStruct((half, 2, rows, columns), jnp.bfloat16),
            jax.ShapeDtypeStruct((8, 128), jnp.float32),
        ],
        scratch_shapes=[pltpu.VMEM((columns, columns), jnp.float32)],
        compiler_params=params(),
        cost_estimate=cost(4 * half * rows * columns * columns, 8 * momentum.size),
        name="packed_grams",
    )(squares, grad_slot, momentum, grads, other_momentum, other_grads)


def momentum_kernel(slot_ref, clip_ref, rows_ref, m_ref, g_ref, out_ref, made_ref, written):
    half = rows_ref.shape[0]
    core = lax.axis_index("slab") % 2
    copies = [
        pltpu.make_async_copy(rows_ref.at[e, 0], out_ref.at[core * half + e], written.at[0, e])
        for e in range(half)
    ]
    for copy in copies:
        copy.start()
    for e in range(half):
        expert = (1 - core) * half + e
        made_ref[e] = fresh_momentum(
            m_ref[expert], slot_gradient(slot_ref[...], expert, g_ref), clip_ref[:1, :1]
        )
        copy = pltpu.make_async_copy(made_ref.at[e], out_ref.at[expert], written.at[1, e])
        copy.start()
        copies.append(copy)
    for copy in copies:
        copy.wait()


def update_momentum(grad_slot, clip, rows, momentum, grads):
    half, _, depth, columns = rows.shape
    return pl.pallas_call(
        momentum_kernel,
        in_specs=[whole(pltpu.VMEM)] * 5,
        out_specs=whole(pltpu.HBM),
        out_shape=jax.ShapeDtypeStruct((2 * half, depth, columns), jnp.bfloat16),
        scratch_shapes=[
            pltpu.VMEM((half, depth, columns), jnp.bfloat16),
            pltpu.SemaphoreType.DMA((2, half)),
        ],
        compiler_params=params(),
        cost_estimate=cost(3 * rows.size, 6 * rows.size),
        name="update_momentum",
    )(grad_slot, clip, rows, momentum, grads)


def bf16_dot(left, right):
    return jnp.dot(left, right, preferred_element_type=jnp.float32)


def scaled_rows(rows, factor):
    return (jnp.sqrt(jnp.float32(M)) * bf16_dot(rows, factor)).astype(jnp.bfloat16)


def lower_product(left, right):
    half = left.shape[0] // 2
    return (
        bf16_dot(left[:half], right[:, :half]),
        bf16_dot(left[half:], right[:, :half]),
        bf16_dot(left[half:], right[:, half:]),
    )


def mirrored(parts):
    upper, corner, lower = (part.astype(jnp.bfloat16) for part in parts)
    return jnp.concatenate(
        [
            jnp.concatenate([upper, corner.T], axis=1),
            jnp.concatenate([corner, lower], axis=1),
        ],
        axis=0,
    )


def unpack_scaled(e, packs, gram_ref, whole_matrix):
    columns = gram_ref.shape[0]
    size = columns // BLOCKS
    row, column = grid_index((size, size))

    def piece(pack, at, end):
        return sum(ref[e, at:end, :].astype(jnp.float32) for ref in pack)

    shared = [piece(pack, 3 * size, 4 * size) for pack in packs]
    diagonal = [piece(pack, 4 * size, 4 * size + TAIL)[:1, :] for pack in packs]
    trace = sum(jnp.sum(jnp.where(column == row, value, 0.0), keepdims=True) for value in shared)
    trace += sum(jnp.sum(value, keepdims=True) for value in diagonal)
    frob = trace + 1e-06
    scale = 1.0 / frob

    def put(i, j, value):
        gram_ref[i * size : (i + 1) * size, j * size : (j + 1) * size] = value

    for at, (lower, (first, second)) in enumerate(HALVES):
        for k, (i, j) in enumerate(lower):
            value = scale * piece(packs[at], k * size, (k + 1) * size)
            put(i, j, value)
            if whole_matrix or i // 2 == j // 2:
                put(j, i, value.T)
        value = scale * shared[at]
        flipped = value.T
        put(first, first, jnp.where(column <= row, value, flipped))
        put(
            second,
            second,
            jnp.where(
                column == row,
                scale * diagonal[at],
                jnp.where(column > row, value, flipped),
            ),
        )
    return frob


def unpack_half(e, refs):
    size = refs[0].shape[2]
    row, column = grid_index((size, size))

    def piece(start, depth):
        return sum(ref[e, start : start + depth, :].astype(jnp.float32) for ref in refs)

    shared = piece(3 * size, size)
    flipped = shared.T
    diagonal = piece(4 * size, TAIL)[:1, :]
    trace = jnp.sum(jnp.where(column == row, shared, 0.0), keepdims=True)
    trace += jnp.sum(diagonal, keepdims=True)
    first = jnp.where(column <= row, shared, flipped)
    last = jnp.where(column == row, diagonal, jnp.where(column > row, shared, flipped))
    return first, last, [piece(at * size, size) for at in range(3)], trace


def quarter(first, lower, last):
    return jnp.concatenate(
        [
            jnp.concatenate([first, lower.T], axis=1),
            jnp.concatenate([lower, last], axis=1),
        ],
        axis=0,
    )


def second_half_kernel(b0_ref, b1_ref, low_ref, corner_ref, trace_ref):
    for e in range(b0_ref.shape[0]):
        first, last, lower, trace = unpack_half(e, (b0_ref, b1_ref))
        low_ref[e] = quarter(first, lower[2], last)
        corner_ref[e] = jnp.concatenate(lower[:2], axis=1)
        trace_ref[e] = jnp.broadcast_to(trace, trace_ref.shape[1:])


def second_half(b0, b1):
    half, _, size = b0.shape
    return pl.pallas_call(
        second_half_kernel,
        in_specs=[whole(pltpu.VMEM)] * 2,
        out_specs=[whole(pltpu.VMEM)] * 3,
        out_shape=[
            jax.ShapeDtypeStruct((half, 2 * size, 2 * size), jnp.float32),
            jax.ShapeDtypeStruct((half, size, 2 * size), jnp.float32),
            jax.ShapeDtypeStruct((half, 8, 128), jnp.float32),
        ],
        compiler_params=params(),
        cost_estimate=cost(4 * b0.size, 12 * b0.size),
        name="second_half",
    )(b0, b1)


def newton_kernel(
    a0_ref, a1_ref, low_ref, corner_ref, trace_ref, rows_ref, factor_ref, send_ref, narrow_ref
):
    e = pl.program_id(0)
    columns = rows_ref.shape[3]
    first, last, lower, trace = unpack_half(e, (a0_ref, a1_ref))
    frob = trace + trace_ref[e][:1, :1] + 1e-06
    scale = 1.0 / frob
    corner = jnp.concatenate([jnp.concatenate(lower[1:], axis=1), corner_ref[e]], axis=0)
    current = (scale * quarter(first, lower[0], last), scale * corner, scale * low_ref[e])
    half = columns // 2
    row, column = grid_index((half, half))
    identity = jnp.where(row == column, COEF_A, 0.0)
    for iteration in range(ITERS):
        rounded = mirrored(current)
        squared = lower_product(rounded, rounded)
        if iteration == 0:
            spread = jnp.sum(jnp.where(row == column, squared[0] + squared[2], 0.0), keepdims=True)
            narrow = jnp.where(spread > SPREAD, 1.0, 0.0)
            narrow_ref[e] = jnp.broadcast_to(narrow, narrow_ref.shape[1:])
        poly = [COEF_B * x + COEF_C * y for x, y in zip(current, squared)]
        poly_half = mirrored((identity + poly[0], poly[1], identity + poly[2]))
        if iteration == 0:
            product = poly_half
        else:
            product = lower_product(product, poly_half)
            if iteration < ITERS - 1:
                product = mirrored(product)
        if iteration < ITERS - 1:
            halfway = mirrored(lower_product(rounded, poly_half))
            current = lower_product(poly_half, halfway)
    scale = lax.rsqrt(frob)
    factor = mirrored([part * scale for part in product])
    factor_ref[e] = factor
    depth = rows_ref.shape[2]
    send_ref[e, :depth] = scaled_rows(rows_ref[e, 1], factor)
    send_ref[e, depth:] = jnp.broadcast_to(narrow, (TAIL, columns)).astype(jnp.bfloat16)


def exact_newton_kernel(
    a0_ref, a1_ref, b0_ref, b1_ref, rows_ref, factor_ref, send_ref, gram_ref
):
    e = pl.program_id(0)
    frob = unpack_scaled(e, ((a0_ref, a1_ref), (b0_ref, b1_ref)), gram_ref, True)
    row, column = grid_index(gram_ref.shape)
    identity = jnp.where(row == column, COEF_A, 0.0)
    current = gram_ref[...]
    for iteration in range(ITERS):
        rounded = current.astype(jnp.bfloat16)
        poly = identity + COEF_B * current + COEF_C * bf16_dot(rounded, rounded)
        poly_half = poly.astype(jnp.bfloat16)
        if iteration == 0:
            product = poly
        else:
            product = bf16_dot(product.astype(jnp.bfloat16), poly_half)
        if iteration < ITERS - 1:
            halfway = bf16_dot(rounded, poly_half).astype(jnp.bfloat16)
            current = bf16_dot(poly_half, halfway)
    factor = (product / jnp.sqrt(frob)).astype(jnp.bfloat16)
    factor_ref[e] = factor
    send_ref[e] = scaled_rows(rows_ref[e, 1], factor)


def newton_factors(terms, rows, exact):
    half, _, depth, columns = rows.shape
    narrow = [] if exact else [jax.ShapeDtypeStruct((half, 8, 128), jnp.float32)]
    return pl.pallas_call(
        exact_newton_kernel if exact else newton_kernel,
        grid=(half,),
        in_specs=[whole(pltpu.VMEM)] * (len(terms) + 1),
        out_specs=[whole(pltpu.VMEM)] * (2 + len(narrow)),
        out_shape=[
            jax.ShapeDtypeStruct((half, columns, columns), jnp.bfloat16),
            jax.ShapeDtypeStruct((half, depth + (0 if exact else TAIL), columns), jnp.bfloat16),
        ]
        + narrow,
        scratch_shapes=[pltpu.VMEM((columns, columns), jnp.float32)] if exact else [],
        compiler_params=params(("arbitrary",)),
        cost_estimate=cost(
            10 * half * columns**3, 2 * (4 * terms[0].size + half * columns * columns)
        ),
        name="exact_newton" if exact else "newton_factors",
    )(*terms, rows)


def own_kernel(rows_ref, factor_ref, *refs):
    out_ref, made_ref, written = refs[-3:]
    half, depth, _ = made_ref.shape
    pieces = written.shape[1]
    size = depth // pieces
    core = lax.axis_index("slab") % 2
    copies = []
    for e in range(half):
        for piece in range(pieces):
            at = pl.ds(piece * size, size)
            made_ref[e, at] = scaled_rows(rows_ref[e, 0, at], factor_ref[e])
            copies.append(
                pltpu.make_async_copy(
                    made_ref.at[e, at], out_ref.at[core * half + e, at], written.at[e, piece]
                )
            )
            copies[-1].start()
    for copy in copies:
        copy.wait()


def update_own(rows, factors, update=None):
    into = () if update is None else (update,)
    half, _, depth, columns = rows.shape
    return pl.pallas_call(
        own_kernel,
        in_specs=[whole(pltpu.VMEM)] * 2 + [whole(pltpu.HBM)] * len(into),
        out_specs=whole(pltpu.HBM),
        out_shape=pltpu.HBM((2 * half, depth, columns), jnp.bfloat16),
        scratch_shapes=[
            pltpu.VMEM((half, depth, columns), jnp.bfloat16),
            pltpu.SemaphoreType.DMA((half, 2)),
        ],
        input_output_aliases={2: 0} if into else {},
        compiler_params=params(),
        cost_estimate=cost(2 * half * depth * columns * columns, 6 * half * depth * columns),
        name="update_own",
    )(rows, factors, *into)


def other_kernel(got_ref, update_ref, out_ref, written):
    half, depth = got_ref.shape[0], out_ref.shape[1]
    other = 1 - lax.axis_index("slab") % 2
    copy = pltpu.make_async_copy(
        got_ref.at[:, pl.ds(0, depth)], out_ref.at[pl.ds(other * half, half)], written
    )
    copy.start()
    return copy


def plain_other_kernel(got_ref, update_ref, out_ref, written):
    other_kernel(got_ref, update_ref, out_ref, written).wait()


def flag_other_kernel(got_ref, update_ref, narrow_ref, out_ref, flag_ref, written):
    copy = other_kernel(got_ref, update_ref, out_ref, written)
    own = jnp.max(jnp.max(narrow_ref[...], axis=0), keepdims=True)
    tails = got_ref[:, got_ref.shape[1] - TAIL :, :128].astype(jnp.float32)
    flag_ref[0, 0] = jnp.max(jnp.maximum(own, jnp.max(jnp.max(tails, axis=0), keepdims=True)))
    copy.wait()


def update_other(got, update, narrow=None):
    written = pltpu.HBM(update.shape, update.dtype)
    common = dict(
        scratch_shapes=[pltpu.SemaphoreType.DMA],
        input_output_aliases={1: 0},
        compiler_params=params(),
        cost_estimate=cost(0, 4 * got.size),
    )
    if narrow is None:
        return pl.pallas_call(
            plain_other_kernel,
            in_specs=[whole(pltpu.VMEM), whole(pltpu.HBM)],
            out_specs=whole(pltpu.HBM),
            out_shape=written,
            name="update_other",
            **common,
        )(got, update)
    return pl.pallas_call(
        flag_other_kernel,
        in_specs=[whole(pltpu.VMEM), whole(pltpu.HBM), whole(pltpu.VMEM)],
        out_specs=[whole(pltpu.HBM), whole(pltpu.SMEM)],
        out_shape=[written, pltpu.SMEM((1, 1), jnp.float32)],
        name="update_other_flag",
        **common,
    )(got, update, narrow)


def add_rounded(left, right):
    return (left.astype(jnp.float32) + right.astype(jnp.float32)).astype(left.dtype)


def on_device(grads, grad_slot, momentum):
    slab_count = lax.axis_size("slab")
    devices = slab_count * lax.axis_size("group")

    def swap(value, bit, odd_bit=None):
        odd_bit = odd_bit or bit
        pairs = [(i, i ^ (odd_bit if i % 2 else bit)) for i in range(slab_count)]
        return lax.ppermute(value, "slab", pairs)

    partial, grad_slot = sum_squares(grads, grad_slot, devices)
    other_momentum, other_grads = swap(momentum, 1), swap(grads, 1)
    squares = lax.all_to_all(partial, AXES, 0, 0, tiled=True)
    a, b, rows, clip = packed_grams(
        squares, grad_slot, momentum, grads, other_momentum, other_grads, grads.size * devices
    )
    bits = []
    while 2 << len(bits) < slab_count:
        bits.append(2 << len(bits))
    turned = bits[len(bits) // 2 :] + bits[: len(bits) // 2]

    def added_up(a, b, beside=None):
        for step, (bit_a, bit_b) in enumerate(zip(bits, turned)):
            a1, b1 = swap(a, bit_a), swap(b, bit_b)
            if step < len(bits) - 1:
                a, b = add_rounded(a, a1), add_rounded(b, b1)
            if step == 0 and beside is not None:
                a, beside = lax.optimization_barrier((a, beside))
        return (a, a1, b, b1), beside

    fresh = update_momentum(grad_slot, clip, rows, momentum, grads)
    terms, fresh = added_up(a, b, fresh)
    terms = (*terms[:2], *second_half(*terms[2:]))
    factors, send, narrow = newton_factors(terms, rows, exact=False)
    got = swap(send, 1)
    update, flag = update_other(got, update_own(rows, factors), narrow)

    def narrow_update(rows, update):
        terms, _ = added_up(*exact_grams(rows))
        factors, send = newton_factors(terms, rows, exact=True)
        return update_other(swap(send, 1), update_own(rows, factors, update))

    def spread_update(rows, update):
        return update

    update = lax.cond(flag[0, 0] > 0.0, narrow_update, spread_update, rows, update)
    return (fresh, update)


def solution(mesh):
    in_specs = (P("group", "slab", None), P("group", None), P("group", "slab", None))
    out_specs = (P("group", "slab", None), P("group", "slab", None))
    return jax.shard_map(
        on_device, mesh=mesh, in_specs=in_specs, out_specs=out_specs, check_vma=False
    )
```

```python
import functools

import jax
import jax.numpy as jnp
from jax import lax
from jax.experimental import pallas as pl
from jax.experimental.pallas import tpu as pltpu
from jax.sharding import PartitionSpec as P

M = 2048
ITERS = 2

COEF_A = 3.4445
COEF_B = -4.775
COEF_C = 2.0315
DECAY_RATE = 0.95

AXES = ("slab", "group")
VMEM_LIMIT = 24 * 1024 * 1024
SPREAD = 0.02
HALVES = (
    (((1, 0), (2, 0), (2, 1)), (0, 1)),
    (((3, 0), (3, 1), (3, 2)), (2, 3)),
)
BLOCKS = 4
TAIL = 16


def params(semantics=None, limit=VMEM_LIMIT):
    return pltpu.CompilerParams(vmem_limit_bytes=limit, dimension_semantics=semantics)


def cost(flops, bytes_accessed):
    return pl.CostEstimate(flops=flops, bytes_accessed=bytes_accessed, transcendentals=0)


def whole(memory_space):
    return pl.BlockSpec(memory_space=memory_space)


def squares_kernel(grads_ref, slot_ref, out_ref, slots_ref):
    slots_ref[...] = slot_ref[...]
    values = grads_ref[...].astype(jnp.float32)
    total = jnp.sum((values * values).reshape(values.shape[0] // 8, 8, -1), axis=0)
    lanes = sum(total[:, at : at + 128] for at in range(0, total.shape[1], 128))
    out_ref[...] = jnp.broadcast_to(jnp.sum(lanes, axis=0, keepdims=True), out_ref.shape)


def sum_squares(grads, grad_slot, copies):
    rows, columns = grads.shape[0] * grads.shape[1], grads.shape[2]
    return pl.pallas_call(
        squares_kernel,
        out_shape=[
            jax.ShapeDtypeStruct((copies, 128), jnp.float32),
            jax.ShapeDtypeStruct(grad_slot.shape, jnp.int32),
        ],
        in_specs=[whole(pltpu.VMEM)] * 2,
        out_specs=[whole(pltpu.VMEM)] * 2,
        compiler_params=params(),
        cost_estimate=cost(2 * grads.size, 2 * grads.size),
        name="sum_squares",
    )(grads.reshape(rows, columns), grad_slot)


def slot_gradient(slots, expert, grads_ref):
    lane = lax.broadcasted_iota(jnp.int32, slots.shape, 1)
    slot = jnp.sum(jnp.where(lane == expert, slots, 0), axis=1, keepdims=True)
    gradient = grads_ref[0]
    for at in range(1, grads_ref.shape[0]):
        gradient = jnp.where(slot == at, grads_ref[at], gradient)
    return gradient


def fresh_momentum(momentum, gradient, clip):
    return (
        DECAY_RATE * momentum.astype(jnp.float32) + clip * gradient.astype(jnp.float32)
    ).astype(jnp.bfloat16)


def grid_index(shape):
    return (
        lax.broadcasted_iota(jnp.int32, shape, 0),
        lax.broadcasted_iota(jnp.int32, shape, 1),
    )


def pack_gram(e, rows_ref, pa_ref, pb_ref, gram_ref):
    _, _, rows, columns = rows_ref.shape
    size = columns // BLOCKS
    row, column = grid_index((size, size))
    fresh = rows_ref[e].reshape(2 * rows, columns)
    middle = columns // 2
    for rows_at, columns_at in ((0, 0), (middle, 0), (middle, middle)):
        gram_ref[rows_at : rows_at + middle, columns_at : columns_at + middle] = lax.dot_general(
            fresh[:, rows_at : rows_at + middle],
            fresh[:, columns_at : columns_at + middle],
            (((0,), (0,)), ((), ())),
            preferred_element_type=jnp.float32,
        )

    def block(i, j):
        return gram_ref[i * size : (i + 1) * size, j * size : (j + 1) * size]

    diagonals = []
    for (lower, (first, second)), out_ref in zip(HALVES, (pa_ref, pb_ref)):
        for at, (i, j) in enumerate(lower):
            out_ref[e, at * size : (at + 1) * size, :] = block(i, j).astype(out_ref.dtype)
        last = block(second, second)
        shared = jnp.where(column <= row, block(first, first), last)
        out_ref[e, 3 * size : 4 * size, :] = shared.astype(out_ref.dtype)
        diagonal = jnp.sum(jnp.where(column == row, last, 0.0), axis=0, keepdims=True)
        diagonals.append(jnp.broadcast_to(diagonal, (TAIL // 2, size)))
    pb_ref[e, 4 * size :, :] = jnp.concatenate(diagonals, axis=0).astype(pb_ref.dtype)


def packed_shapes(half, size, dtype):
    return [jax.ShapeDtypeStruct((half, 4 * size + tail, size), dtype) for tail in (0, TAIL)]


def exact_grams_kernel(rows_ref, pa_ref, pb_ref, gram_ref):
    pack_gram(pl.program_id(0), rows_ref, pa_ref, pb_ref, gram_ref)


def exact_grams(rows):
    half, _, depth, columns = rows.shape
    size = columns // BLOCKS
    return pl.pallas_call(
        exact_grams_kernel,
        grid=(half,),
        in_specs=[whole(pltpu.VMEM)],
        out_specs=[whole(pltpu.VMEM)] * 2,
        out_shape=packed_shapes(half, size, jnp.float32),
        scratch_shapes=[pltpu.VMEM((columns, columns), jnp.float32)],
        compiler_params=params(("arbitrary",)),
        cost_estimate=cost(4 * half * depth * columns * columns, 4 * rows.size),
        name="exact_grams",
    )(rows)


def gram_kernel(
    entries, squares_ref, slot_ref, m_ref, g_ref, om_ref, og_ref,
    pa_ref, pb_ref, rows_ref, clip_ref, gram_ref,
):
    total = jnp.sum(squares_ref[...], keepdims=True)
    root_mean = jnp.sqrt(total / entries + 1e-06)
    clip = jnp.minimum(1.0, 1.0 / root_mean)
    clip_ref[...] = jnp.broadcast_to(clip, clip_ref.shape)
    half = m_ref.shape[0] // 2
    core = lax.axis_index("slab") % 2
    for e in range(half):
        expert = core * half + e
        for at, (momentum_ref, grads_ref) in enumerate(((m_ref, g_ref), (om_ref, og_ref))):
            rows_ref[e, at] = fresh_momentum(
                momentum_ref[expert], slot_gradient(slot_ref[...], expert, grads_ref), clip
            )
        pack_gram(e, rows_ref, pa_ref, pb_ref, gram_ref)


def packed_grams(squares, grad_slot, momentum, grads, other_momentum, other_grads, entries):
    experts, rows, columns = momentum.shape
    half = experts // 2
    size = columns // BLOCKS
    return pl.pallas_call(
        functools.partial(gram_kernel, entries),
        in_specs=[whole(pltpu.VMEM)] * 6,
        out_specs=[whole(pltpu.VMEM)] * 4,
        out_shape=packed_shapes(half, size, jnp.bfloat16)
        + [
            jax.ShapeDtypeStruct((half, 2, rows, columns), jnp.bfloat16),
            jax.ShapeDtypeStruct((8, 128), jnp.float32),
        ],
        scratch_shapes=[pltpu.VMEM((columns, columns), jnp.float32)],
        compiler_params=params(),
        cost_estimate=cost(4 * half * rows * columns * columns, 8 * momentum.size),
        name="packed_grams",
    )(squares, grad_slot, momentum, grads, other_momentum, other_grads)


def momentum_kernel(slot_ref, clip_ref, rows_ref, m_ref, g_ref, out_ref, made_ref, written):
    half = rows_ref.shape[0]
    core = lax.axis_index("slab") % 2
    copies = [
        pltpu.make_async_copy(rows_ref.at[e, 0], out_ref.at[core * half + e], written.at[0, e])
        for e in range(half)
    ]
    for copy in copies:
        copy.start()
    for e in range(half):
        expert = (1 - core) * half + e
        made_ref[e] = fresh_momentum(
            m_ref[expert], slot_gradient(slot_ref[...], expert, g_ref), clip_ref[:1, :1]
        )
        copy = pltpu.make_async_copy(made_ref.at[e], out_ref.at[expert], written.at[1, e])
        copy.start()
        copies.append(copy)
    for copy in copies:
        copy.wait()


def update_momentum(grad_slot, clip, rows, momentum, grads):
    half, _, depth, columns = rows.shape
    return pl.pallas_call(
        momentum_kernel,
        in_specs=[whole(pltpu.VMEM)] * 5,
        out_specs=whole(pltpu.HBM),
        out_shape=jax.ShapeDtypeStruct((2 * half, depth, columns), jnp.bfloat16),
        scratch_shapes=[
            pltpu.VMEM((half, depth, columns), jnp.bfloat16),
            pltpu.SemaphoreType.DMA((2, half)),
        ],
        compiler_params=params(),
        cost_estimate=cost(3 * rows.size, 6 * rows.size),
        name="update_momentum",
    )(grad_slot, clip, rows, momentum, grads)


def bf16_dot(left, right):
    return jnp.dot(left, right, preferred_element_type=jnp.float32)


def scaled_rows(rows, factor):
    return (jnp.sqrt(jnp.float32(M)) * bf16_dot(rows, factor)).astype(jnp.bfloat16)


def lower_product(left, right):
    half = left.shape[0] // 2
    return (
        bf16_dot(left[:half], right[:, :half]),
        bf16_dot(left[half:], right[:, :half]),
        bf16_dot(left[half:], right[:, half:]),
    )


def mirrored(parts):
    upper, corner, lower = (part.astype(jnp.bfloat16) for part in parts)
    return jnp.concatenate(
        [
            jnp.concatenate([upper, corner.T], axis=1),
            jnp.concatenate([corner, lower], axis=1),
        ],
        axis=0,
    )


def unpack_scaled(e, packs, gram_ref, whole_matrix):
    columns = gram_ref.shape[0]
    size = columns // BLOCKS
    row, column = grid_index((size, size))

    def piece(pack, at, end):
        return sum(ref[e, at:end, :].astype(jnp.float32) for ref in pack)

    shared = [piece(pack, 3 * size, 4 * size) for pack in packs]
    tail = piece(packs[1], 4 * size, 4 * size + TAIL)
    diagonal = [tail[:1, :], tail[TAIL // 2 : TAIL // 2 + 1, :]]
    trace = sum(jnp.sum(jnp.where(column == row, value, 0.0), keepdims=True) for value in shared)
    trace += sum(jnp.sum(value, keepdims=True) for value in diagonal)
    frob = trace + 1e-06
    scale = 1.0 / frob

    def put(i, j, value):
        gram_ref[i * size : (i + 1) * size, j * size : (j + 1) * size] = value

    for at, (lower, (first, second)) in enumerate(HALVES):
        for k, (i, j) in enumerate(lower):
            value = scale * piece(packs[at], k * size, (k + 1) * size)
            put(i, j, value)
            if whole_matrix or i // 2 == j // 2:
                put(j, i, value.T)
        value = scale * shared[at]
        flipped = value.T
        put(first, first, jnp.where(column <= row, value, flipped))
        put(
            second,
            second,
            jnp.where(
                column == row,
                scale * diagonal[at],
                jnp.where(column > row, value, flipped),
            ),
        )
    return frob


def unpack_half(e, refs, diagonal):
    size = refs[0].shape[2]
    row, column = grid_index((size, size))

    def piece(start, depth):
        return sum(ref[e, start : start + depth, :].astype(jnp.float32) for ref in refs)

    shared = piece(3 * size, size)
    flipped = shared.T
    trace = jnp.sum(jnp.where(column == row, shared, 0.0), keepdims=True)
    trace += jnp.sum(diagonal, keepdims=True)
    first = jnp.where(column <= row, shared, flipped)
    last = jnp.where(column == row, diagonal, jnp.where(column > row, shared, flipped))
    return first, last, [piece(at * size, size) for at in range(3)], trace


def quarter(first, lower, last):
    return jnp.concatenate(
        [
            jnp.concatenate([first, lower.T], axis=1),
            jnp.concatenate([lower, last], axis=1),
        ],
        axis=0,
    )


def second_half_kernel(b0_ref, b1_ref, low_ref, corner_ref, trace_ref, diagonal_ref):
    for e in range(b0_ref.shape[0]):
        tail = sum(ref[e, ref.shape[1] - TAIL :, :].astype(jnp.float32) for ref in (b0_ref, b1_ref))
        diagonal_ref[e] = tail[: TAIL // 2]
        diagonal = tail[TAIL // 2 : TAIL // 2 + 1, :]
        first, last, lower, trace = unpack_half(e, (b0_ref, b1_ref), diagonal)
        low_ref[e] = quarter(first, lower[2], last)
        corner_ref[e] = jnp.concatenate(lower[:2], axis=1)
        trace_ref[e] = jnp.broadcast_to(trace, trace_ref.shape[1:])


def second_half(b0, b1):
    half, _, size = b0.shape
    return pl.pallas_call(
        second_half_kernel,
        in_specs=[whole(pltpu.VMEM)] * 2,
        out_specs=[whole(pltpu.VMEM)] * 4,
        out_shape=[
            jax.ShapeDtypeStruct((half, 2 * size, 2 * size), jnp.float32),
            jax.ShapeDtypeStruct((half, size, 2 * size), jnp.float32),
            jax.ShapeDtypeStruct((half, 8, 128), jnp.float32),
            jax.ShapeDtypeStruct((half, TAIL // 2, size), jnp.float32),
        ],
        compiler_params=params(),
        cost_estimate=cost(4 * b0.size, 12 * b0.size),
        name="second_half",
    )(b0, b1)


def newton_kernel(
    a0_ref,
    a1_ref,
    low_ref,
    corner_ref,
    trace_ref,
    diagonal_ref,
    rows_ref,
    factor_ref,
    send_ref,
    narrow_ref,
):
    e = pl.program_id(0)
    columns = rows_ref.shape[3]
    first, last, lower, trace = unpack_half(e, (a0_ref, a1_ref), diagonal_ref[e][:1, :])
    frob = trace + trace_ref[e][:1, :1] + 1e-06
    scale = 1.0 / frob
    corner = jnp.concatenate([jnp.concatenate(lower[1:], axis=1), corner_ref[e]], axis=0)
    current = (scale * quarter(first, lower[0], last), scale * corner, scale * low_ref[e])
    half = columns // 2
    row, column = grid_index((half, half))
    identity = jnp.where(row == column, COEF_A, 0.0)
    for iteration in range(ITERS):
        rounded = mirrored(current)
        squared = lower_product(rounded, rounded)
        if iteration == 0:
            spread = jnp.sum(jnp.where(row == column, squared[0] + squared[2], 0.0), keepdims=True)
            narrow = jnp.where(spread > SPREAD, 1.0, 0.0)
            narrow_ref[e] = jnp.broadcast_to(narrow, narrow_ref.shape[1:])
        poly = [COEF_B * x + COEF_C * y for x, y in zip(current, squared)]
        poly_half = mirrored((identity + poly[0], poly[1], identity + poly[2]))
        if iteration == 0:
            product = poly_half
        else:
            product = lower_product(product, poly_half)
            if iteration < ITERS - 1:
                product = mirrored(product)
        if iteration < ITERS - 1:
            halfway = mirrored(lower_product(rounded, poly_half))
            current = lower_product(poly_half, halfway)
    scale = lax.rsqrt(frob)
    factor = mirrored([part * scale for part in product])
    factor_ref[e] = factor
    depth = rows_ref.shape[2]
    send_ref[e, :depth] = scaled_rows(rows_ref[e, 1], factor)
    send_ref[e, depth:] = jnp.broadcast_to(narrow, (TAIL, columns)).astype(jnp.bfloat16)


def exact_newton_kernel(
    a0_ref, a1_ref, b0_ref, b1_ref, rows_ref, factor_ref, send_ref, gram_ref
):
    e = pl.program_id(0)
    frob = unpack_scaled(e, ((a0_ref, a1_ref), (b0_ref, b1_ref)), gram_ref, True)
    row, column = grid_index(gram_ref.shape)
    identity = jnp.where(row == column, COEF_A, 0.0)
    current = gram_ref[...]
    for iteration in range(ITERS):
        rounded = current.astype(jnp.bfloat16)
        poly = identity + COEF_B * current + COEF_C * bf16_dot(rounded, rounded)
        poly_half = poly.astype(jnp.bfloat16)
        if iteration == 0:
            product = poly
        else:
            product = bf16_dot(product.astype(jnp.bfloat16), poly_half)
        if iteration < ITERS - 1:
            halfway = bf16_dot(rounded, poly_half).astype(jnp.bfloat16)
            current = bf16_dot(poly_half, halfway)
    factor = (product / jnp.sqrt(frob)).astype(jnp.bfloat16)
    factor_ref[e] = factor
    send_ref[e] = scaled_rows(rows_ref[e, 1], factor)


def newton_factors(terms, rows, exact):
    half, _, depth, columns = rows.shape
    narrow = [] if exact else [jax.ShapeDtypeStruct((half, 8, 128), jnp.float32)]
    return pl.pallas_call(
        exact_newton_kernel if exact else newton_kernel,
        grid=(half,),
        in_specs=[whole(pltpu.VMEM)] * (len(terms) + 1),
        out_specs=[whole(pltpu.VMEM)] * (2 + len(narrow)),
        out_shape=[
            jax.ShapeDtypeStruct((half, columns, columns), jnp.bfloat16),
            jax.ShapeDtypeStruct((half, depth + (0 if exact else TAIL), columns), jnp.bfloat16),
        ]
        + narrow,
        scratch_shapes=[pltpu.VMEM((columns, columns), jnp.float32)] if exact else [],
        compiler_params=params(("arbitrary",)),
        cost_estimate=cost(
            10 * half * columns**3, 2 * (4 * terms[0].size + half * columns * columns)
        ),
        name="exact_newton" if exact else "newton_factors",
    )(*terms, rows)


def own_kernel(rows_ref, factor_ref, *refs):
    out_ref, made_ref, written = refs[-3:]
    half, depth, _ = made_ref.shape
    pieces = written.shape[1]
    size = depth // pieces
    core = lax.axis_index("slab") % 2
    copies = []
    for e in range(half):
        for piece in range(pieces):
            at = pl.ds(piece * size, size)
            made_ref[e, at] = scaled_rows(rows_ref[e, 0, at], factor_ref[e])
            copies.append(
                pltpu.make_async_copy(
                    made_ref.at[e, at], out_ref.at[core * half + e, at], written.at[e, piece]
                )
            )
            copies[-1].start()
    for copy in copies:
        copy.wait()


def update_own(rows, factors, update=None):
    into = () if update is None else (update,)
    half, _, depth, columns = rows.shape
    return pl.pallas_call(
        own_kernel,
        in_specs=[whole(pltpu.VMEM)] * 2 + [whole(pltpu.HBM)] * len(into),
        out_specs=whole(pltpu.HBM),
        out_shape=pltpu.HBM((2 * half, depth, columns), jnp.bfloat16),
        scratch_shapes=[
            pltpu.VMEM((half, depth, columns), jnp.bfloat16),
            pltpu.SemaphoreType.DMA((half, 2)),
        ],
        input_output_aliases={2: 0} if into else {},
        compiler_params=params(),
        cost_estimate=cost(2 * half * depth * columns * columns, 6 * half * depth * columns),
        name="update_own",
    )(rows, factors, *into)


def other_kernel(got_ref, update_ref, out_ref, written):
    half, depth = got_ref.shape[0], out_ref.shape[1]
    other = 1 - lax.axis_index("slab") % 2
    copy = pltpu.make_async_copy(
        got_ref.at[:, pl.ds(0, depth)], out_ref.at[pl.ds(other * half, half)], written
    )
    copy.start()
    return copy


def plain_other_kernel(got_ref, update_ref, out_ref, written):
    other_kernel(got_ref, update_ref, out_ref, written).wait()


def flag_other_kernel(got_ref, update_ref, narrow_ref, out_ref, flag_ref, written):
    copy = other_kernel(got_ref, update_ref, out_ref, written)
    own = jnp.max(jnp.max(narrow_ref[...], axis=0), keepdims=True)
    tails = got_ref[:, got_ref.shape[1] - TAIL :, :128].astype(jnp.float32)
    flag_ref[0, 0] = jnp.max(jnp.maximum(own, jnp.max(jnp.max(tails, axis=0), keepdims=True)))
    copy.wait()


def update_other(got, update, narrow=None):
    written = pltpu.HBM(update.shape, update.dtype)
    common = dict(
        scratch_shapes=[pltpu.SemaphoreType.DMA],
        input_output_aliases={1: 0},
        compiler_params=params(),
        cost_estimate=cost(0, 4 * got.size),
    )
    if narrow is None:
        return pl.pallas_call(
            plain_other_kernel,
            in_specs=[whole(pltpu.VMEM), whole(pltpu.HBM)],
            out_specs=whole(pltpu.HBM),
            out_shape=written,
            name="update_other",
            **common,
        )(got, update)
    return pl.pallas_call(
        flag_other_kernel,
        in_specs=[whole(pltpu.VMEM), whole(pltpu.HBM), whole(pltpu.VMEM)],
        out_specs=[whole(pltpu.HBM), whole(pltpu.SMEM)],
        out_shape=[written, pltpu.SMEM((1, 1), jnp.float32)],
        name="update_other_flag",
        **common,
    )(got, update, narrow)


def add_rounded(left, right):
    return (left.astype(jnp.float32) + right.astype(jnp.float32)).astype(left.dtype)


def on_device(grads, grad_slot, momentum):
    slab_count = lax.axis_size("slab")
    devices = slab_count * lax.axis_size("group")

    def swap(value, bit, odd_bit=None):
        odd_bit = odd_bit or bit
        pairs = [(i, i ^ (odd_bit if i % 2 else bit)) for i in range(slab_count)]
        return lax.ppermute(value, "slab", pairs)

    partial, grad_slot = sum_squares(grads, grad_slot, devices)
    other_momentum, other_grads = swap(momentum, 1), swap(grads, 1)
    squares = lax.all_to_all(partial, AXES, 0, 0, tiled=True)
    a, b, rows, clip = packed_grams(
        squares, grad_slot, momentum, grads, other_momentum, other_grads, grads.size * devices
    )
    bits = []
    while 2 << len(bits) < slab_count:
        bits.append(2 << len(bits))
    turned = bits[len(bits) // 2 :] + bits[: len(bits) // 2]

    def added_up(a, b, beside=None):
        for step, (bit_a, bit_b) in enumerate(zip(bits, turned)):
            a1, b1 = swap(a, bit_a), swap(b, bit_b)
            if step < len(bits) - 1:
                a, b = add_rounded(a, a1), add_rounded(b, b1)
            if step == 0 and beside is not None:
                a, beside = lax.optimization_barrier((a, beside))
        return (a, a1, b, b1), beside

    fresh = update_momentum(grad_slot, clip, rows, momentum, grads)
    terms, fresh = added_up(a, b, fresh)
    terms = (*terms[:2], *second_half(*terms[2:]))
    factors, send, narrow = newton_factors(terms, rows, exact=False)
    got = swap(send, 1)
    update, flag = update_other(got, update_own(rows, factors), narrow)

    def narrow_update(rows, update):
        terms, _ = added_up(*exact_grams(rows))
        factors, send = newton_factors(terms, rows, exact=True)
        return update_other(swap(send, 1), update_own(rows, factors, update))

    def spread_update(rows, update):
        return update

    update = lax.cond(flag[0, 0] > 0.0, narrow_update, spread_update, rows, update)
    return (fresh, update)


def solution(mesh):
    in_specs = (P("group", "slab", None), P("group", None), P("group", "slab", None))
    out_specs = (P("group", "slab", None), P("group", "slab", None))
    return jax.shard_map(
        on_device, mesh=mesh, in_specs=in_specs, out_specs=out_specs, check_vma=False
    )
```
